32 devices in a mesh: stn: 8 (over z, core), seg: 4 (over y, x).
Axes of the slice: x: 2, y: 2, z: 4, core: 2. Of those that a mesh axis runs over, the one named last changes fastest.
Arguments:
- traces: float32 [1024, 19200], P(('stn', 'seg')), may hold values from -6 to 6
- fir_taps: float32 [31], replicated, may hold values from -0.9 to 0.9
- seg_flags: int32 [1024, 32], P(('stn', 'seg')), may hold values 0 or 1
- pair_mask: int32 [1024, 1024], P('stn', 'seg'), may hold values 0 or 1
Outputs:
- stacked: float32 [41, 1024, 1024], P(None, 'stn', 'seg')
The draws below stay inside these ranges and needn't reach their ends.
All inputs are finite; a program needn't handle non-finite values. No bound on the sum of `seg_flags` or of `pair_mask` on one device may be relied on, other than what follows from the above.
Results may differ from the reference program's by a relative error of at most 0.0095.
Values may be sent and summed in bfloat16 or wider, within the bound.
No kernel may reach another device: no remote copies, remote signals or barrier semaphores. Data moves between devices by JAX's collectives and lax.ppermute only.
A program may use at most 192 MiB of HBM per device.

```python
import math
import jax
import jax.numpy as jnp
from jax import lax

STATIONS = 1024
SAMP = 600
LAGS = 41
TAPS = 31
RADIUS = 64
SEG_DEV = 8
SEGMENTS = 32
N_SEG = 4


def place_ends(array, key, smallest, largest):
    longest = array.shape.index(max(array.shape))
    spots = []
    for shift in (0, 1):
        where = [jax.random.randint(jax.random.fold_in(key, axis), (), 0, length) for axis, length in enumerate(array.shape)]
        where[longest] = (where[longest] + shift) % array.shape[longest]
        spots.append(tuple(where))
    return array.at[spots[0]].set(smallest).at[spots[1]].set(largest)


def shard_levels(own_key, extent, split, low, largest):
    def one(axis_at, blocks):
        heights = jax.random.uniform(jax.random.fold_in(jax.random.fold_in(own_key, 6), axis_at), (blocks,), jnp.float32, low / len(split), largest / len(split))
        return jnp.repeat(jnp.exp(heights), extent[axis_at] // blocks).reshape((-1,) + (1,) * (len(extent) - axis_at - 1))

    factor_of = one(*split[0])
    for cut in split[1:]:
        factor_of = factor_of * one(*cut)
    return factor_of


def noise(stream_key, extent, deviation, bound, cuts=(), held_as=jnp.bfloat16):
    values = deviation * jax.random.normal(stream_key, extent, jnp.float32)
    if cuts:
        values = values * shard_levels(stream_key, extent, cuts, -0.22, 0.18)
    return jnp.clip(values, -bound, bound).astype(held_as)


def setup_inputs(seed: int = 0) -> dict:
    streams_of = jax.random.split(jax.random.key(seed), 5)
    return {
        "traces": noise(streams_of[0], (STATIONS, SEGMENTS * SAMP), 1.0, 6.0, ((0, 32),), jnp.float32),
        "fir_taps": noise(streams_of[1], (TAPS,), 0.3, 0.9, (), jnp.float32),
        "seg_flags": place_ends((jax.random.randint(streams_of[2], (STATIONS, SEGMENTS), 0, 8) < 7).astype(jnp.int32), jax.random.fold_in(streams_of[2], 1), 0, 1),
        "pair_mask": place_ends((jax.random.randint(streams_of[3], (STATIONS, STATIONS), 0, 4) < 3).astype(jnp.int32), jax.random.fold_in(streams_of[3], 1), 0, 1),
    }


epsilon = 1e-06
lag_group = 8

def preprocess(traces, fir_taps, seg_flags):
    station_count = traces.shape[0]
    record_len = traces.shape[1]
    half_taps = (TAPS - 1) // 2
    padded = jnp.pad(traces, ((0, 0), (half_taps, half_taps)))
    filtered = jnp.zeros_like(traces)
    for tap_index in range(TAPS):
        filtered = filtered + fir_taps[tap_index] * padded[:, tap_index:tap_index + record_len]
    width = 2 * RADIUS + 1
    magnitude = jnp.pad(jnp.abs(filtered), ((0, 0), (RADIUS + 1, RADIUS)))
    running = jnp.cumsum(magnitude, axis=1)
    running_level = (running[:, width:] - running[:, :record_len]) / width
    whitened = filtered / (running_level + epsilon)
    flagged = whitened.reshape(station_count, -1, SAMP) * seg_flags[:, :, None].astype(jnp.float32)
    return flagged.astype(jnp.bfloat16)

def correlate(left_rows, right_rows):
    half_lag = (LAGS - 1) // 2
    row_count = left_rows.shape[0]
    right_flat = right_rows.reshape(right_rows.shape[0], -1)
    left_padded = jnp.pad(left_rows, ((0, 0), (0, 0), (half_lag, half_lag)))
    results = []
    for first_lag in range(0, LAGS, lag_group):
        lag_list = list(range(first_lag, min(first_lag + lag_group, LAGS)))
        shifted = jnp.stack([left_padded[:, :, LAGS - 1 - lag_index:LAGS - 1 - lag_index + SAMP] for lag_index in lag_list], axis=0)
        shifted = shifted.reshape(len(lag_list) * row_count, -1)
        product = lax.dot_general(shifted, right_flat, (((1,), (1,)), ((), ())), preferred_element_type=jnp.float32)
        results.append(product.reshape(len(lag_list), row_count, right_flat.shape[0]))
    return jnp.concatenate(results, axis=0)

def reference(traces, fir_taps, seg_flags, pair_mask):
    whitened = preprocess(traces, fir_taps, seg_flags)
    norm_scale = 1.0 / math.sqrt(SAMP * SEGMENTS)
    stacked = jnp.zeros((LAGS, STATIONS, STATIONS), jnp.float32)
    for group_index in range(N_SEG):
        group_rows = whitened[:, group_index * SEG_DEV:(group_index + 1) * SEG_DEV]
        group_part = (correlate(group_rows, group_rows) * norm_scale).astype(jnp.bfloat16)
        stacked = stacked + lax.optimization_barrier(group_part).astype(jnp.float32)
    return stacked * pair_mask.astype(jnp.float32)[None]
```

```python
import functools
import math

import jax
import jax.numpy as jnp
from jax import lax
from jax.experimental import pallas as pl
from jax.experimental.pallas import tpu as pltpu
from jax.sharding import PartitionSpec as P

SAMP = 600
LAGS = 41
TAPS = 31
RADIUS = 64
LANES = 128
HALF_LAG = (LAGS - 1) // 2
HALF_TAPS = (TAPS - 1) // 2

epsilon = 1e-06
chunk_segs = 8
lag_group = 7
vmem_bytes = 58 << 20


def split_bf16(value):
    high = value.astype(jnp.bfloat16)
    low = (value - high.astype(jnp.float32)).astype(jnp.bfloat16)
    return high, low


def dot_f32(left, right):
    return jnp.dot(left, right, preferred_element_type=jnp.float32)


def whiten_kernel(chunk_len, taps_ref, traces_ref, flags_ref, *out_refs):
    rows, record_len = traces_ref.shape
    blocks = record_len // LANES
    traces = traces_ref[...]
    stacked = jnp.concatenate(
        [jnp.zeros((rows, LANES), jnp.float32)]
        + [traces[:, j * LANES : (j + 1) * LANES] for j in range(blocks)]
        + [jnp.zeros((2 * rows, LANES), jnp.float32)],
        axis=0,
    )

    def windows(value):
        return jnp.concatenate([value[:-rows], value[rows:]], axis=1)

    offset = lax.broadcasted_iota(jnp.int32, (2 * LANES, LANES), 0) - lax.broadcasted_iota(
        jnp.int32, (2 * LANES, LANES), 1
    )
    band = jnp.zeros((2 * LANES, LANES), jnp.float32)
    for tap_index in range(TAPS):
        band = jnp.where(offset == tap_index, taps_ref[tap_index], band)
    late_band = jnp.concatenate(
        [jnp.zeros((RADIUS, LANES), jnp.float32), band[: 2 * LANES - RADIUS]], axis=0
    )
    band_high, band_low = split_bf16(jnp.concatenate([band, late_band], axis=1))
    high, low = split_bf16(stacked)
    high, low = windows(high), windows(low)
    both = dot_f32(high, band_high) + dot_f32(low, band_high) + dot_f32(high, band_low)

    magnitude = jnp.abs(both[:, :LANES])
    lane = lax.broadcasted_iota(jnp.int32, (rows, LANES), 1)
    magnitude = jnp.concatenate(
        [
            jnp.where(lane >= LANES - HALF_TAPS, magnitude[:rows], 0.0),
            magnitude[rows : blocks * rows],
            jnp.where(
                lane < LANES - HALF_TAPS, magnitude[blocks * rows : (blocks + 1) * rows], 0.0
            ),
            jnp.zeros((rows, LANES), jnp.float32),
        ],
        axis=0,
    )
    ones = jnp.where((offset >= 0) & (offset <= 2 * RADIUS), 1.0, 0.0).astype(jnp.bfloat16)
    high, low = split_bf16(magnitude)
    level = (dot_f32(windows(high), ones) + dot_f32(windows(low), ones)) * (1.0 / (2 * RADIUS + 1))
    filtered = both[: (blocks + 1) * rows, LANES:]
    whitened = filtered / (level + epsilon)

    shift = LANES - HALF_TAPS - RADIUS
    moved = pltpu.roll(whitened, LANES - shift, 1)
    lane = lax.broadcasted_iota(jnp.int32, (blocks * rows, LANES), 1)
    aligned = jnp.where(lane < LANES - shift, moved[: blocks * rows], moved[rows:])
    flat = jnp.concatenate([aligned[j * rows : (j + 1) * rows] for j in range(blocks)], axis=1)

    segments = flags_ref.shape[1]
    first = SAMP * lax.broadcasted_iota(jnp.int32, (segments, record_len), 0)
    sample = lax.broadcasted_iota(jnp.int32, (segments, record_len), 1)
    inside = jnp.where((sample >= first) & (sample < first + SAMP), 1.0, 0.0).astype(jnp.bfloat16)
    kept = dot_f32(flags_ref[...].astype(jnp.float32).astype(jnp.bfloat16), inside)
    flat = (flat * kept).astype(jnp.bfloat16)
    for index, out_ref in enumerate(out_refs):
        out_ref[...] = flat[:, index * chunk_len : (index + 1) * chunk_len]


def whiten(traces, fir_taps, seg_flags, chunk_count):
    rows, record_len = traces.shape
    chunk_len = record_len // chunk_count
    vmem = pl.BlockSpec(memory_space=pltpu.VMEM)
    return pl.pallas_call(
        functools.partial(whiten_kernel, chunk_len),
        in_specs=[pl.BlockSpec(memory_space=pltpu.SMEM), vmem, vmem],
        out_specs=[vmem] * chunk_count,
        out_shape=[jax.ShapeDtypeStruct((rows, chunk_len), jnp.bfloat16)] * chunk_count,
        compiler_params=pltpu.CompilerParams(vmem_limit_bytes=vmem_bytes),
        name="whiten",
    )(fir_taps, traces, seg_flags)


def route_kernel(place_ref, *refs):
    count = len(refs) // 2
    for index, out_ref in enumerate(refs[count:]):
        for source_index, source in enumerate(refs[:count]):

            @pl.when(place_ref[index] == source_index)
            def _(source=source, out_ref=out_ref):
                out_ref[...] = source[...]


def route(place, pieces):
    vmem = pl.BlockSpec(memory_space=pltpu.VMEM)
    return pl.pallas_call(
        route_kernel,
        in_specs=[pl.BlockSpec(memory_space=pltpu.SMEM)] + [vmem] * len(pieces),
        out_specs=[vmem] * len(pieces),
        out_shape=[jax.ShapeDtypeStruct(p.shape, p.dtype) for p in pieces],
        compiler_params=pltpu.CompilerParams(vmem_limit_bytes=vmem_bytes),
        name="route",
    )(place, *pieces)


def correlate_kernel(seg_count, sides, has_total, last, scale, place_ref, *refs):
    refs = list(refs)
    left = [refs.pop(0) for _ in range(seg_count)]
    right = [refs.pop(0) for _ in range(seg_count * sides)]
    total_ref = refs.pop(0) if has_total else None
    mask_ref = refs.pop(0) if last else None
    out_ref, moved, columns, shifted = refs[:4]
    piece_rows, chunk_len = left[0].shape
    row_count, padded_len = moved.shape
    step = pl.program_id(0)

    @pl.when(step == 0)
    def _():
        edge = chunk_len // LANES * LANES
        if padded_len > chunk_len:
            moved[:, edge:] = jnp.zeros((row_count, padded_len - edge), moved.dtype)
            columns[:, edge:] = jnp.zeros((columns.shape[0], padded_len - edge), columns.dtype)
        for index, piece in enumerate(left):
            moved[index * piece_rows : (index + 1) * piece_rows, :chunk_len] = piece[...]
        staged = refs[4] if len(refs) > 4 else columns
        for index, piece in enumerate(right):
            at = pl.multiple_of(place_ref[seg_count + index] * piece_rows, piece_rows)
            staged[pl.ds(at, piece_rows), :chunk_len] = piece[...].astype(staged.dtype)
        if len(refs) > 4:
            columns[:, :chunk_len] = staged[:, :chunk_len].astype(columns.dtype)
        moved[...] = pltpu.roll(moved[...], padded_len - HALF_LAG, 1)

    sample = lax.broadcasted_iota(jnp.int32, (16, padded_len), 1)
    phase = sample
    for segment in range(1, chunk_len // SAMP):
        phase = jnp.where(sample >= segment * SAMP, sample - segment * SAMP, phase)
    phase = jnp.where(sample >= chunk_len, -SAMP, phase)
    base = moved[...]
    for index in range(lag_group):
        lag = step * lag_group + index - HALF_LAG
        rolled = pltpu.roll(base, index, 1) if index else base
        keep = jnp.where((phase >= lag) & (phase < SAMP + lag), 1.0, 0.0).astype(jnp.bfloat16)
        keep = jnp.concatenate([keep] * (row_count // 16), axis=0)
        shifted[index * row_count : (index + 1) * row_count, :] = rolled * keep
    moved[...] = pltpu.roll(base, lag_group, 1)
    product = lax.dot_general(
        shifted[...], columns[...], (((1,), (1,)), ((), ())), preferred_element_type=jnp.float32
    )
    product = product.reshape(lag_group, row_count, columns.shape[0])
    if has_total:
        product = product + total_ref[...]
    if not last:
        out_ref[...] = product
        return
    for index in range(seg_count):
        at = pl.ds(pl.multiple_of(place_ref[index] * piece_rows, piece_rows), piece_rows)
        weight = mask_ref[at, :].astype(jnp.float32) * scale
        out_ref[:, at, :] = product[:, index * piece_rows : (index + 1) * piece_rows] * weight[None]


def correlate(place, left, right, total, mask, last, scale):
    seg_count = len(left)
    piece_rows, chunk_len = left[0].shape
    rows, cols = seg_count * piece_rows, len(right) * piece_rows
    padded_len = pl.cdiv(chunk_len, LANES) * LANES
    whole = pl.BlockSpec((piece_rows, chunk_len), lambda step: (0, 0))
    block = pl.BlockSpec((lag_group, rows, cols), lambda step: (step, 0, 0))
    operands, specs = [place, *left, *right], [pl.BlockSpec(memory_space=pltpu.SMEM)]
    specs += [whole] * (len(left) + len(right))
    aliases = {}
    if total is not None:
        aliases = {len(operands): 0}
        operands.append(total)
        specs.append(block)
    if last:
        operands.append(mask)
        specs.append(pl.BlockSpec((rows, cols), lambda step: (0, 0)))
    scratch = [
        pltpu.VMEM((rows, padded_len), jnp.bfloat16),
        pltpu.VMEM((cols, padded_len), jnp.bfloat16),
        pltpu.VMEM((lag_group * rows, padded_len), jnp.bfloat16),
    ]
    if piece_rows % 16:
        scratch.append(pltpu.VMEM((cols, padded_len), jnp.float32))
    return pl.pallas_call(
        functools.partial(
            correlate_kernel, seg_count, len(right) // seg_count, total is not None, last, scale
        ),
        grid=(pl.cdiv(LAGS, lag_group),),
        in_specs=specs,
        out_specs=block,
        out_shape=jax.ShapeDtypeStruct((LAGS, rows, cols), jnp.float32),
        input_output_aliases=aliases,
        scratch_shapes=scratch,
        compiler_params=pltpu.CompilerParams(vmem_limit_bytes=vmem_bytes),
        cost_estimate=pl.CostEstimate(
            flops=2 * LAGS * rows * cols * chunk_len,
            bytes_accessed=8 * LAGS * rows * cols + 2 * (rows + cols) * chunk_len,
            transcendentals=0,
        ),
        name="correlate",
    )(*operands)


def body(traces, fir_taps, seg_flags, pair_mask):
    stn_count, seg_count = lax.axis_size("stn"), lax.axis_size("seg")
    sides = stn_count // seg_count
    stn, seg = lax.axis_index("stn"), lax.axis_index("seg")
    plane, side = stn // sides, stn % sides
    segments = seg_flags.shape[1]
    chunk_count = segments // chunk_segs
    scale = 1.0 / math.sqrt(SAMP * segments)
    partner = jnp.stack([seg ^ k for k in range(seg_count)]).astype(jnp.int32)
    route_place = plane ^ partner
    place = jnp.concatenate(
        [partner] + [(side ^ j) * seg_count + partner for j in range(sides)]
    ).astype(jnp.int32)

    def to_seg(value, k):
        return lax.ppermute(value, "seg", [(i, i ^ k) for i in range(seg_count)])

    def to_plane(value, k):
        return lax.ppermute(value, "stn", [(i, i ^ (k * sides)) for i in range(stn_count)])

    def to_side(value, j):
        return lax.ppermute(value, "stn", [(i, i ^ j) for i in range(stn_count)])

    pieces = whiten(traces, fir_taps, seg_flags, chunk_count)
    total = None
    for index, piece in enumerate(pieces):
        line = [piece]
        for k in range(1, seg_count):
            low = k & (k - 1)
            line.append(to_plane(line[k ^ low] if low else piece, low or k))
        left = [piece] + [to_seg(piece, k) for k in range(1, seg_count)]
        routed = route(route_place, line)
        own = [routed[0]] + [to_seg(routed[k], k) for k in range(1, seg_count)]
        right = own + [to_side(value, j) for j in range(1, sides) for value in own]
        last = index == chunk_count - 1
        total = correlate(place, left, right, total, pair_mask, last, scale)
    return total


def solution(mesh):
    return jax.shard_map(
        body,
        mesh=mesh,
        in_specs=(P(("stn", "seg"), None), P(), P(("stn", "seg"), None), P("stn", "seg")),
        out_specs=P(None, "stn", "seg"),
        check_vma=False,
    )
```

```python
import functools
import math

import jax
import jax.numpy as jnp
from jax import lax
from jax.experimental import pallas as pl
from jax.experimental.pallas import tpu as pltpu
from jax.sharding import PartitionSpec as P

SAMP = 600
LAGS = 41
TAPS = 31
RADIUS = 64
LANES = 128
HALF_LAG = (LAGS - 1) // 2
HALF_TAPS = (TAPS - 1) // 2

epsilon = 1e-06
chunk_segs = 8
lag_group = 7
vmem_bytes = 58 << 20


def split_bf16(value):
    high = value.astype(jnp.bfloat16)
    low = (value - high.astype(jnp.float32)).astype(jnp.bfloat16)
    return high, low


def dot_f32(left, right):
    return jnp.dot(left, right, preferred_element_type=jnp.float32)


def whiten_kernel(starts, taps_ref, traces_ref, flags_ref, *out_refs):
    rows, record_len = traces_ref.shape
    blocks = record_len // LANES
    traces = traces_ref[...]
    stacked = jnp.concatenate(
        [jnp.zeros((rows, LANES), jnp.float32)]
        + [traces[:, j * LANES : (j + 1) * LANES] for j in range(blocks)]
        + [jnp.zeros((2 * rows, LANES), jnp.float32)],
        axis=0,
    )

    def windows(value):
        return jnp.concatenate([value[:-rows], value[rows:]], axis=1)

    offset = lax.broadcasted_iota(jnp.int32, (2 * LANES, LANES), 0) - lax.broadcasted_iota(
        jnp.int32, (2 * LANES, LANES), 1
    )
    band = jnp.zeros((2 * LANES, LANES), jnp.float32)
    for tap_index in range(TAPS):
        band = jnp.where(offset == tap_index, taps_ref[tap_index], band)
    late_band = jnp.concatenate(
        [jnp.zeros((RADIUS, LANES), jnp.float32), band[: 2 * LANES - RADIUS]], axis=0
    )
    band_high, band_low = split_bf16(jnp.concatenate([band, late_band], axis=1))
    high, low = split_bf16(stacked)
    high, low = windows(high), windows(low)
    both = dot_f32(high, band_high) + dot_f32(low, band_high) + dot_f32(high, band_low)

    magnitude = jnp.abs(both[:, :LANES])
    lane = lax.broadcasted_iota(jnp.int32, (rows, LANES), 1)
    magnitude = jnp.concatenate(
        [
            jnp.where(lane >= LANES - HALF_TAPS, magnitude[:rows], 0.0),
            magnitude[rows : blocks * rows],
            jnp.where(
                lane < LANES - HALF_TAPS, magnitude[blocks * rows : (blocks + 1) * rows], 0.0
            ),
            jnp.zeros((rows, LANES), jnp.float32),
        ],
        axis=0,
    )
    ones = jnp.where((offset >= 0) & (offset <= 2 * RADIUS), 1.0, 0.0).astype(jnp.bfloat16)
    high, low = split_bf16(magnitude)
    level = (dot_f32(windows(high), ones) + dot_f32(windows(low), ones)) * (1.0 / (2 * RADIUS + 1))
    filtered = both[: (blocks + 1) * rows, LANES:]
    whitened = filtered / (level + epsilon)

    shift = LANES - HALF_TAPS - RADIUS
    moved = pltpu.roll(whitened, LANES - shift, 1)
    lane = lax.broadcasted_iota(jnp.int32, (blocks * rows, LANES), 1)
    aligned = jnp.where(lane < LANES - shift, moved[: blocks * rows], moved[rows:])
    flat = jnp.concatenate([aligned[j * rows : (j + 1) * rows] for j in range(blocks)], axis=1)

    segments = flags_ref.shape[1]
    first = SAMP * lax.broadcasted_iota(jnp.int32, (segments, record_len), 0)
    sample = lax.broadcasted_iota(jnp.int32, (segments, record_len), 1)
    inside = jnp.where((sample >= first) & (sample < first + SAMP), 1.0, 0.0).astype(jnp.bfloat16)
    kept = dot_f32(flags_ref[...].astype(jnp.float32).astype(jnp.bfloat16), inside)
    flat = (flat * kept).astype(jnp.bfloat16)
    for start, out_ref in zip(starts, out_refs):
        out_ref[...] = flat[:, start : start + out_ref.shape[1]]


def whiten(traces, fir_taps, seg_flags, spans):
    vmem = pl.BlockSpec(memory_space=pltpu.VMEM)
    return pl.pallas_call(
        functools.partial(whiten_kernel, [start for start, _ in spans]),
        in_specs=[pl.BlockSpec(memory_space=pltpu.SMEM), vmem, vmem],
        out_specs=[vmem] * len(spans),
        out_shape=[jax.ShapeDtypeStruct((traces.shape[0], length), jnp.bfloat16) for _, length in spans],
        compiler_params=pltpu.CompilerParams(vmem_limit_bytes=vmem_bytes),
        name="whiten",
    )(fir_taps, traces, seg_flags)


def route_kernel(place_ref, *refs):
    count = len(refs) // 2
    for index, out_ref in enumerate(refs[count:]):
        for source_index, source in enumerate(refs[:count]):

            @pl.when(place_ref[index] == source_index)
            def _(source=source, out_ref=out_ref):
                out_ref[...] = source[...]


def route(place, parts, rows):
    length = parts[0][0].shape[1]
    kind = parts[0][0].dtype
    return pl.pallas_call(
        route_kernel,
        grid=(1,),
        in_specs=[pl.BlockSpec(memory_space=pltpu.SMEM)]
        + [pl.BlockSpec((rows, length), functools.partial(lambda at, step: (at, 0), at)) for _, at in parts],
        out_specs=[pl.BlockSpec((rows, length), lambda step: (0, 0))] * len(parts),
        out_shape=[jax.ShapeDtypeStruct((rows, length), kind)] * len(parts),
        compiler_params=pltpu.CompilerParams(vmem_limit_bytes=vmem_bytes),
        name="route",
    )(place, *[array for array, _ in parts])


def correlate_kernel(start, left_count, has_total, last, scale, place_ref, *refs):
    lefts, refs = refs[:left_count], list(refs[left_count:])
    piece_rows, chunk_len = refs[0].shape
    staged = refs.pop() if piece_rows % 16 else None
    *refs, out_ref, moved, columns, shifted, sems = refs
    staged = columns if staged is None else staged
    mask_ref = refs.pop() if last else None
    total_ref = refs.pop() if has_total else None
    row_count, padded_len = moved.shape
    step = pl.program_id(0)
    begin = start // LANES * LANES

    @pl.when(step == 0)
    def _():
        copies = [
            pltpu.make_async_copy(
                left.at[:, pl.ds(begin, padded_len)],
                moved.at[pl.ds(index * left.shape[0], left.shape[0])],
                sems.at[index],
            )
            for index, left in enumerate(lefts)
        ]
        for copy in copies:
            copy.start()
        edge = chunk_len // LANES * LANES
        if padded_len > chunk_len:
            columns[:, edge:] = jnp.zeros((columns.shape[0], padded_len - edge), columns.dtype)
        for index, piece in enumerate(refs):
            at = pl.multiple_of(place_ref[index] * piece_rows, piece_rows)
            staged[pl.ds(at, piece_rows), :chunk_len] = piece[...].astype(staged.dtype)
        if staged is not columns:
            columns[:, :chunk_len] = staged[:, :chunk_len].astype(columns.dtype)
        for copy in copies:
            copy.wait()
        moved[...] = pltpu.roll(moved[...], padded_len - HALF_LAG - (start - begin), 1)

    sample = lax.broadcasted_iota(jnp.int32, (16, padded_len), 1)
    phase = sample
    for segment in range(1, chunk_len // SAMP):
        phase = jnp.where(sample >= segment * SAMP, sample - segment * SAMP, phase)
    phase = jnp.where(sample >= chunk_len, -SAMP, phase)
    base = moved[...]
    for index in range(lag_group):
        lag = step * lag_group + index - HALF_LAG
        rolled = pltpu.roll(base, index, 1) if index else base
        keep = jnp.where((phase >= lag) & (phase < SAMP + lag), 1.0, 0.0).astype(jnp.bfloat16)
        keep = jnp.concatenate([keep] * (row_count // 16), axis=0)
        shifted[index * row_count : (index + 1) * row_count, :] = rolled * keep
    moved[...] = pltpu.roll(base, lag_group, 1)
    product = lax.dot_general(
        shifted[...], columns[...], (((1,), (1,)), ((), ())), preferred_element_type=jnp.float32
    )
    product = product.reshape(lag_group, row_count, columns.shape[0])
    if has_total:
        product = product + total_ref[...]
    if not last:
        out_ref[...] = product
        return
    for index, left in enumerate(lefts):
        rows = left.shape[0]
        at = pl.ds(pl.multiple_of(place_ref[len(refs) + index] * rows, rows), rows)
        weight = mask_ref[at, :].astype(jnp.float32) * scale
        out_ref[:, at, :] = product[:, index * rows : (index + 1) * rows] * weight[None]


def correlate(place, lefts, start, right, total, mask, last, scale):
    rows = sum(left.shape[0] for left in lefts)
    piece_rows, chunk_len = right[0].shape
    cols = len(right) * piece_rows
    padded_len = pl.cdiv(chunk_len, LANES) * LANES
    whole = pl.BlockSpec((piece_rows, chunk_len), lambda step: (0, 0))
    block = pl.BlockSpec((lag_group, rows, cols), lambda step: (step, 0, 0))
    operands = [place, *lefts, *right]
    specs = [pl.BlockSpec(memory_space=pltpu.SMEM)] + [pl.BlockSpec(memory_space=pl.ANY)] * len(lefts)
    specs += [whole] * len(right)
    aliases = {}
    if total is not None:
        aliases = {len(operands): 0}
        operands.append(total)
        specs.append(block)
    if last:
        operands.append(mask)
        specs.append(pl.BlockSpec((rows, cols), lambda step: (0, 0)))
    scratch = [
        pltpu.VMEM((rows, padded_len), jnp.bfloat16),
        pltpu.VMEM((cols, padded_len), jnp.bfloat16),
        pltpu.VMEM((lag_group * rows, padded_len), jnp.bfloat16),
        pltpu.SemaphoreType.DMA((len(lefts),)),
    ]
    if piece_rows % 16:
        scratch.append(pltpu.VMEM((cols, padded_len), jnp.float32))
    return pl.pallas_call(
        functools.partial(correlate_kernel, start, len(lefts), total is not None, last, scale),
        grid=(pl.cdiv(LAGS, lag_group),),
        in_specs=specs,
        out_specs=block,
        out_shape=jax.ShapeDtypeStruct((LAGS, rows, cols), jnp.float32),
        input_output_aliases=aliases,
        scratch_shapes=scratch,
        compiler_params=pltpu.CompilerParams(vmem_limit_bytes=vmem_bytes),
        name="correlate",
    )(*operands)


def body(traces, fir_taps, seg_flags, pair_mask):
    stn_count, seg_count = lax.axis_size("stn"), lax.axis_size("seg")
    sides = stn_count // seg_count
    stn, seg = lax.axis_index("stn"), lax.axis_index("seg")
    plane, side = stn // sides, stn % sides
    segments = seg_flags.shape[1]
    count = segments // chunk_segs
    scale = 1.0 / math.sqrt(SAMP * segments)
    partner = jnp.stack([seg ^ k for k in range(seg_count)]).astype(jnp.int32)
    route_place = plane ^ partner
    rows = traces.shape[0]
    place = [(side ^ j) * seg_count + partner for j in range(sides)]

    def to_seg(value, k):
        return lax.ppermute(value, "seg", [(i, i ^ k) for i in range(seg_count)])

    def to_plane(value, k):
        return lax.ppermute(value, "stn", [(i, i ^ (k * sides)) for i in range(stn_count)])

    def to_side(value, j):
        return lax.ppermute(value, "stn", [(i, i ^ j) for i in range(stn_count)])

    length = chunk_segs * SAMP
    record_len = traces.shape[1]
    half_len = record_len // 2
    spans = [(u * length, length) for u in range(count)] + [(0, half_len), (half_len, half_len)]
    *units, early, late = whiten(traces, fir_taps, seg_flags, spans)
    direct = [k for k in range(1, seg_count) if k & (k - 1) == 0][::-1]
    passed = [k for k in range(1, seg_count) if k & (k - 1)]
    gathered = rows % 16 > 0
    place.append(jnp.zeros((1,), jnp.int32) if gathered else partner)
    place = jnp.concatenate(place).astype(jnp.int32)

    state = {("unit", u): unit for u, unit in enumerate(units)}
    state["early", 0], state["late", 0] = early, late
    lines = [{0: (("unit", u), 0)} for u in range(count)]

    def fence():
        names = list(state)
        state.update(zip(names, lax.optimization_barrier([state[n] for n in names])))

    def value(u, k):
        name, at = lines[u][k]
        return state[name][at * rows : (at + 1) * rows] if at else state[name][:rows]

    def hop(k, *moves):
        sent = [value(u, slot ^ k) for u, slot in moves]
        name = ("line", *moves)
        state[name] = to_plane(jnp.concatenate(sent, axis=0) if len(sent) > 1 else sent[0], k)
        for at, (u, slot) in enumerate(moves):
            lines[u][slot] = name, at

    def plane_hops(u):
        ahead = u + 1 < count
        if len(passed) == 1 and u >= 0:
            if ahead:
                hop(direct[0], (u + 1, direct[0]))
            if u < count:
                hop(direct[1], *([(u, passed[0])] + ([(u + 1, direct[1])] if ahead else [])))
            return
        for k in passed if 0 <= u < count else []:
            hop(k & (k - 1), (u, k))
        for k in direct if ahead else []:
            hop(k, (u + 1, k))

    def columns(u):
        parts = [(state[lines[u][k][0]], lines[u][k][1]) for k in range(seg_count)]
        for k, piece in enumerate(route(route_place, parts, rows)):
            state["own", u, k] = to_seg(piece, k) if k else piece

    def row_hops(name, which):
        if not gathered:
            for k in which:
                state[name, k] = to_seg(state[name, 0], k)
        elif which:
            state[name, 0] = lax.all_gather(state[name, 0], "seg", axis=0, tiled=True)

    def products(u):
        name, start = ("early", u * length) if u < count // 2 else ("late", u * length - half_len)
        lefts = [state[name, k] for k in range(1 if gathered else seg_count)]
        own = [state.pop(("own", u, k)) for k in range(seg_count)]
        right = own + [to_side(v, j) for j in range(1, sides) for v in own]
        state["total"] = correlate(
            place, lefts, start, right, state.pop("total", None), pair_mask, u == count - 1, scale
        )

    near, far = list(range(1, seg_count - 1)), [seg_count - 1]
    plane_hops(-1)
    row_hops("early", near)
    for u in range(count + 2):
        fence()
        plane_hops(u)
        if 1 <= u <= count:
            columns(u - 1)
        if u == 0:
            row_hops("early", [] if gathered else far)
            row_hops("late", near)
        if u == count // 2 + 1:
            row_hops("late", [] if gathered else far)
        if 2 <= u <= count:
            products(u - 2)
    products(count - 1)
    return state["total"]


def solution(mesh):
    return jax.shard_map(
        body,
        mesh=mesh,
        in_specs=(P(("stn", "seg"), None), P(), P(("stn", "seg"), None), P("stn", "seg")),
        out_specs=P(None, "stn", "seg"),
        check_vma=False,
    )
```

```python
import functools
import math

import jax
import jax.numpy as jnp
from jax import lax
from jax.experimental import pallas as pl
from jax.experimental.pallas import tpu as pltpu
from jax.sharding import PartitionSpec as P

SAMP = 600
LAGS = 41
TAPS = 31
RADIUS = 64
LANES = 128
HALF_LAG = (LAGS - 1) // 2
HALF_TAPS = (TAPS - 1) // 2

epsilon = 1e-06
chunk_segs = 8
lag_group = 7
vmem_bytes = 58 << 20


def split_bf16(value):
    high = value.astype(jnp.bfloat16)
    low = (value - high.astype(jnp.float32)).astype(jnp.bfloat16)
    return high, low


def dot_f32(left, right):
    return jnp.dot(left, right, preferred_element_type=jnp.float32)


def whiten_kernel(record_tiles, first, starts, taps_ref, traces_ref, flags_ref, *out_refs):
    rows = traces_ref.shape[0]
    blocks = max(start + out.shape[1] for start, out in zip(starts, out_refs)) // LANES - first

    def tile(j):
        if j < 0 or j >= record_tiles:
            return jnp.zeros((rows, LANES), jnp.float32)
        return traces_ref[:, j * LANES : (j + 1) * LANES]

    stacked = jnp.concatenate([tile(first + j - 1) for j in range(blocks + 3)], axis=0)

    def windows(value):
        return jnp.concatenate([value[:-rows], value[rows:]], axis=1)

    offset = lax.broadcasted_iota(jnp.int32, (2 * LANES, LANES), 0) - lax.broadcasted_iota(
        jnp.int32, (2 * LANES, LANES), 1
    )
    band = jnp.zeros((2 * LANES, LANES), jnp.float32)
    for tap_index in range(TAPS):
        band = jnp.where(offset == tap_index, taps_ref[tap_index], band)
    late_band = jnp.concatenate(
        [jnp.zeros((RADIUS, LANES), jnp.float32), band[: 2 * LANES - RADIUS]], axis=0
    )
    band_high, band_low = split_bf16(jnp.concatenate([band, late_band], axis=1))
    high, low = split_bf16(stacked)
    high, low = windows(high), windows(low)
    both = dot_f32(high, band_high) + dot_f32(low, band_high) + dot_f32(high, band_low)

    magnitude = jnp.abs(both[:, :LANES])
    lane = lax.broadcasted_iota(jnp.int32, (rows, LANES), 1)
    last = record_tiles - first

    def inside_record(j):
        value = magnitude[j * rows : (j + 1) * rows]
        if first + j == 0:
            return jnp.where(lane >= LANES - HALF_TAPS, value, 0.0)
        if j >= last:
            return jnp.where(lane < LANES - HALF_TAPS, value, 0.0) if j == last else jnp.zeros_like(value)
        return value

    magnitude = jnp.concatenate([inside_record(j) for j in range(blocks + 2)], axis=0)
    ones = jnp.where((offset >= 0) & (offset <= 2 * RADIUS), 1.0, 0.0).astype(jnp.bfloat16)
    high, low = split_bf16(magnitude)
    level = (dot_f32(windows(high), ones) + dot_f32(windows(low), ones)) * (1.0 / (2 * RADIUS + 1))
    filtered = both[: (blocks + 1) * rows, LANES:]
    whitened = filtered / (level + epsilon)

    shift = LANES - HALF_TAPS - RADIUS
    moved = pltpu.roll(whitened, LANES - shift, 1)
    lane = lax.broadcasted_iota(jnp.int32, (blocks * rows, LANES), 1)
    aligned = jnp.where(lane < LANES - shift, moved[: blocks * rows], moved[rows:])
    flat = jnp.concatenate([aligned[j * rows : (j + 1) * rows] for j in range(blocks)], axis=1)

    segments = flags_ref.shape[1]
    at = lax.broadcasted_iota(jnp.int32, (segments, blocks * LANES), 1) + first * LANES
    at -= SAMP * lax.broadcasted_iota(jnp.int32, (segments, blocks * LANES), 0)
    inside = jnp.where((at >= 0) & (at < SAMP), 1.0, 0.0).astype(jnp.bfloat16)
    kept = dot_f32(flags_ref[...].astype(jnp.float32).astype(jnp.bfloat16), inside)
    flat = (flat * kept).astype(jnp.bfloat16)
    for start, out_ref in zip(starts, out_refs):
        start -= first * LANES
        out_ref[...] = flat[:, start : start + out_ref.shape[1]]


def whiten(traces, fir_taps, seg_flags, spans):
    rows, record_len = traces.shape
    vmem = pl.BlockSpec(memory_space=pltpu.VMEM)
    first = min(start for start, _ in spans) // LANES
    reach = min(max(start + length for start, length in spans) + 2 * LANES, record_len)
    return pl.pallas_call(
        functools.partial(whiten_kernel, record_len // LANES, first, [start for start, _ in spans]),
        grid=(1,),
        in_specs=[
            pl.BlockSpec(memory_space=pltpu.SMEM),
            pl.BlockSpec((rows, reach), lambda step: (0, 0)),
            vmem,
        ],
        out_specs=[vmem] * len(spans),
        out_shape=[jax.ShapeDtypeStruct((rows, length), jnp.bfloat16) for _, length in spans],
        compiler_params=pltpu.CompilerParams(vmem_limit_bytes=vmem_bytes),
        name="whiten",
    )(fir_taps, traces, seg_flags)


def route_kernel(place_ref, *refs):
    count = len(refs) // 2
    for index, out_ref in enumerate(refs[count:]):
        for source_index, source in enumerate(refs[:count]):

            @pl.when(place_ref[index] == source_index)
            def _(source=source, out_ref=out_ref):
                out_ref[...] = source[...]


def route(place, parts, rows):
    length = parts[0][0].shape[1]
    kind = parts[0][0].dtype
    return pl.pallas_call(
        route_kernel,
        grid=(1,),
        in_specs=[pl.BlockSpec(memory_space=pltpu.SMEM)]
        + [pl.BlockSpec((rows, length), functools.partial(lambda at, step: (at, 0), at)) for _, at in parts],
        out_specs=[pl.BlockSpec((rows, length), lambda step: (0, 0))] * len(parts),
        out_shape=[jax.ShapeDtypeStruct((rows, length), kind)] * len(parts),
        compiler_params=pltpu.CompilerParams(vmem_limit_bytes=vmem_bytes),
        name="route",
    )(place, *[array for array, _ in parts])


def correlate_kernel(offset, begins, left_count, has_total, last, scale, place_ref, *refs):
    lefts, refs = refs[:left_count], list(refs[left_count:])
    piece_rows, padded_len = refs[0].shape
    staged = refs.pop() if piece_rows % 16 else None
    *refs, out_ref, moved, columns, shifted, sems = refs
    mask_ref = refs.pop() if last else None
    total_ref = refs.pop() if has_total else None
    row_count = moved.shape[0]
    step = pl.program_id(0)

    @pl.when(step == 0)
    def _():
        copies = []

        def copy(source, target):
            copies.append(pltpu.make_async_copy(source, target, sems.at[len(copies)]))
            copies[-1].start()

        for index, left in enumerate(lefts):
            rows = left.shape[0]
            copy(left.at[:, pl.ds(begins[index], padded_len)], moved.at[pl.ds(index * rows, rows)])
        for index, piece in enumerate(refs):
            at = pl.ds(pl.multiple_of(place_ref[index] * piece_rows, piece_rows), piece_rows)
            if staged is None:
                copy(piece, columns.at[at])
            else:
                staged[at, :] = piece[...].astype(staged.dtype)
        if staged is not None:
            columns[...] = staged[...].astype(columns.dtype)
        for started in copies:
            started.wait()
        moved[...] = pltpu.roll(moved[...], padded_len - HALF_LAG, 1)

    sample = lax.broadcasted_iota(jnp.int32, (16, padded_len), 1) - offset
    phase = jnp.where(sample < 0, -SAMP, sample)
    for segment in range(1, chunk_segs):
        phase = jnp.where(sample >= segment * SAMP, sample - segment * SAMP, phase)
    phase = jnp.where(sample >= chunk_segs * SAMP, -SAMP, phase)
    base = moved[...]
    for index in range(lag_group):
        lag = step * lag_group + index - HALF_LAG
        rolled = pltpu.roll(base, index, 1) if index else base
        keep = jnp.where((phase >= lag) & (phase < SAMP + lag), 1.0, 0.0).astype(jnp.bfloat16)
        keep = jnp.concatenate([keep] * (row_count // 16), axis=0)
        shifted[index * row_count : (index + 1) * row_count, :] = rolled * keep
    moved[...] = pltpu.roll(base, lag_group, 1)
    product = lax.dot_general(
        shifted[...], columns[...], (((1,), (1,)), ((), ())), preferred_element_type=jnp.float32
    )
    product = product.reshape(lag_group, row_count, columns.shape[0])
    if has_total:
        product = product + total_ref[...]
    if not last:
        out_ref[...] = product
        return
    for index, left in enumerate(lefts):
        rows = left.shape[0]
        at = pl.ds(pl.multiple_of(place_ref[len(refs) + index] * rows, rows), rows)
        weight = mask_ref[at, :].astype(jnp.float32) * scale
        out_ref[:, at, :] = product[:, index * rows : (index + 1) * rows] * weight[None]


def correlate(place, lefts, begins, offset, right, total, mask, last, scale):
    rows = sum(left.shape[0] for left in lefts)
    piece_rows, padded_len = right[0].shape
    cols = len(right) * piece_rows
    any_space = pl.BlockSpec(memory_space=pl.ANY)
    whole = pl.BlockSpec((piece_rows, padded_len), lambda step: (0, 0)) if piece_rows % 16 else any_space
    block = pl.BlockSpec((lag_group, rows, cols), lambda step: (step, 0, 0))
    operands = [place, *lefts, *right]
    specs = [pl.BlockSpec(memory_space=pltpu.SMEM)] + [any_space] * len(lefts)
    specs += [whole] * len(right)
    aliases = {}
    if total is not None:
        aliases = {len(operands): 0}
        operands.append(total)
        specs.append(block)
    if last:
        operands.append(mask)
        specs.append(pl.BlockSpec((rows, cols), lambda step: (0, 0)))
    scratch = [
        pltpu.VMEM((rows, padded_len), jnp.bfloat16),
        pltpu.VMEM((cols, padded_len), jnp.bfloat16),
        pltpu.VMEM((lag_group * rows, padded_len), jnp.bfloat16),
        pltpu.SemaphoreType.DMA((len(lefts) + len(right),)),
    ]
    if piece_rows % 16:
        scratch.append(pltpu.VMEM((cols, padded_len), jnp.float32))
    return pl.pallas_call(
        functools.partial(correlate_kernel, offset, begins, len(lefts), total is not None, last, scale),
        grid=(pl.cdiv(LAGS, lag_group),),
        in_specs=specs,
        out_specs=block,
        out_shape=jax.ShapeDtypeStruct((LAGS, rows, cols), jnp.float32),
        input_output_aliases=aliases,
        scratch_shapes=scratch,
        compiler_params=pltpu.CompilerParams(vmem_limit_bytes=vmem_bytes),
        name="correlate",
    )(*operands)


def body(traces, fir_taps, seg_flags, pair_mask):
    stn_count, seg_count = lax.axis_size("stn"), lax.axis_size("seg")
    sides = stn_count // seg_count
    stn, seg = lax.axis_index("stn"), lax.axis_index("seg")
    plane, side = stn // sides, stn % sides
    segments = seg_flags.shape[1]
    count = segments // chunk_segs
    scale = 1.0 / math.sqrt(SAMP * segments)
    partner = jnp.stack([seg ^ k for k in range(seg_count)]).astype(jnp.int32)
    route_place = plane ^ partner
    rows = traces.shape[0]
    place = [(side ^ j) * seg_count + partner for j in range(sides)]

    def to_seg(value, k):
        return lax.ppermute(value, "seg", [(i, i ^ k) for i in range(seg_count)])

    def to_plane(value, k):
        return lax.ppermute(value, "stn", [(i, i ^ (k * sides)) for i in range(stn_count)])

    def to_side(value, j):
        return lax.ppermute(value, "stn", [(i, i ^ j) for i in range(stn_count)])

    length = chunk_segs * SAMP
    window = pl.cdiv(length, LANES) * LANES
    begins = [u * length // LANES * LANES for u in range(count)]
    half = count // 2
    middle = begins[1], pl.cdiv((half + 1) * length, LANES) * LANES - begins[1]
    late = begins[half], traces.shape[1] - begins[half]
    units = list(whiten(traces, fir_taps, seg_flags, [(begins[0], window)]))
    spans = [(begin, window) for begin in begins[1:]] + [middle, late]
    *rest, middle, late = whiten(traces, fir_taps, seg_flags, spans)
    units += rest

    direct = [k for k in range(1, seg_count) if k & (k - 1) == 0][::-1]
    passed = [k for k in range(1, seg_count) if k & (k - 1)]
    gathered = rows % 16 > 0
    place.append(jnp.zeros((1,), jnp.int32) if gathered else partner)
    place = jnp.concatenate(place).astype(jnp.int32)

    state = {("unit", u): unit for u, unit in enumerate(units)}
    state["middle"], state["late"] = middle, late
    lines = [{0: (("unit", u), 0)} for u in range(count)]

    def fence():
        names = list(state)
        state.update(zip(names, lax.optimization_barrier([state[n] for n in names])))

    def value(u, k):
        name, at = lines[u][k]
        return state[name][at * rows : (at + 1) * rows] if at else state[name][:rows]

    def hop(k, *moves):
        sent = [value(u, slot ^ k) for u, slot in moves]
        name = ("line", *moves)
        state[name] = to_plane(jnp.concatenate(sent, axis=0) if len(sent) > 1 else sent[0], k)
        for at, (u, slot) in enumerate(moves):
            lines[u][slot] = name, at

    def plane_hops(u):
        ahead = u + 1 < count
        if len(passed) == 1 and u >= 0:
            if ahead:
                hop(direct[0], (u + 1, direct[0]))
            if u < count:
                hop(direct[1], *([(u, passed[0])] + ([(u + 1, direct[1])] if ahead else [])))
            return
        for k in passed if 0 <= u < count else []:
            hop(k & (k - 1), (u, k))
        for k in direct if ahead else []:
            hop(k, (u + 1, k))

    def columns(u):
        parts = [(state[lines[u][k][0]], lines[u][k][1]) for k in range(seg_count)]
        for k, piece in enumerate(route(route_place, parts, rows)):
            state["own", u, k] = to_seg(piece, k) if k else piece

    rows_of = [{0: (("unit", u), 0)} for u in range(count)]

    def row_hop(k, source, covered):
        name = ("row", k, source)
        state[name] = to_seg(state[source], k)
        for u in covered:
            rows_of[u][k] = name, 0 if source == ("unit", u) else begins[u] - begins[covered[0]]

    def gather_rows(source, covered):
        name = ("rows", source)
        state[name] = lax.all_gather(state[source], "seg", axis=0, tiled=True)
        for u in covered:
            rows_of[u] = {0: (name, begins[u] - begins[covered[0]])}

    def products(u):
        parts = [rows_of[u][k] for k in sorted(rows_of[u])]
        own = [state.pop(("own", u, k)) for k in range(seg_count)]
        right = own + [to_side(v, j) for j in range(1, sides) for v in own]
        state["total"] = correlate(
            place,
            [state[name] for name, _ in parts],
            [begin for _, begin in parts],
            u * length - begins[u],
            right,
            state.pop("total", None),
            pair_mask,
            u == count - 1,
            scale,
        )

    hops = list(range(1, seg_count))
    row_plan = {
        -1: [(k, ("unit", 0), [0]) for k in hops],
        0: [(k, "middle", range(1, half + 1)) for k in hops[:-1]] + [(hops[-1], ("unit", 1), [1])],
        half + 1: [(hops[-1], "late", range(half, count))],
    }
    for v in range(half + 1, count):
        row_plan[v + 1] = row_plan.get(v + 1, []) + [(k, ("unit", v), [v]) for k in hops[:-1]]
    plane_hops(-1)
    if gathered:
        for source, covered in ((("unit", 0), [0]), ("middle", range(1, half)), ("late", range(half, count))):
            gather_rows(source, list(covered))
        row_plan = {}
    for u in range(-1, count + 2):
        if u >= 0:
            fence()
            plane_hops(u)
        if 1 <= u <= count:
            columns(u - 1)
        for k, source, covered in row_plan.get(u, []):
            row_hop(k, source, list(covered))
        if 2 <= u <= count:
            products(u - 2)
    products(count - 1)
    return state["total"]


def solution(mesh):
    return jax.shard_map(
        body,
        mesh=mesh,
        in_specs=(P(("stn", "seg"), None), P(), P(("stn", "seg"), None), P("stn", "seg")),
        out_specs=P(None, "stn", "seg"),
        check_vma=False,
    )
```

```python
import functools
import math

import jax
import jax.numpy as jnp
from jax import lax
from jax.experimental import pallas as pl
from jax.experimental.pallas import tpu as pltpu
from jax.sharding import PartitionSpec as P

SAMP = 600
LAGS = 41
TAPS = 31
RADIUS = 64
LANES = 128
HALF_LAG = (LAGS - 1) // 2
SHIFTS = HALF_LAG + 1
HALF_TAPS = (TAPS - 1) // 2

epsilon = 1e-06
chunk_segs = 8
shift_group = 7
vmem_bytes = 58 << 20


def split_bf16(value):
    high = value.astype(jnp.bfloat16)
    low = (value - high.astype(jnp.float32)).astype(jnp.bfloat16)
    return high, low


def dot_f32(left, right):
    return jnp.dot(left, right, preferred_element_type=jnp.float32)


def whiten_kernel(record_tiles, first, blocks, starts, taps_ref, traces_ref, flags_ref, *out_refs):
    rows = traces_ref.shape[0]

    def tile(j):
        if j < 0 or j >= record_tiles:
            return jnp.zeros((rows, LANES), jnp.float32)
        return traces_ref[:, j * LANES : (j + 1) * LANES]

    stacked = jnp.concatenate([tile(first + j - 1) for j in range(blocks + 3)], axis=0)

    def windows(value):
        return jnp.concatenate([value[:-rows], value[rows:]], axis=1)

    offset = lax.broadcasted_iota(jnp.int32, (2 * LANES, LANES), 0) - lax.broadcasted_iota(
        jnp.int32, (2 * LANES, LANES), 1
    )
    band = jnp.zeros((2 * LANES, LANES), jnp.float32)
    for tap_index in range(TAPS):
        band = jnp.where(offset == tap_index, taps_ref[tap_index], band)
    late_band = jnp.concatenate(
        [jnp.zeros((RADIUS, LANES), jnp.float32), band[: 2 * LANES - RADIUS]], axis=0
    )
    band_high, band_low = split_bf16(jnp.concatenate([band, late_band], axis=1))
    high, low = split_bf16(stacked)
    high, low = windows(high), windows(low)
    both = dot_f32(high, band_high) + dot_f32(low, band_high) + dot_f32(high, band_low)

    magnitude = jnp.abs(both[:, :LANES])
    lane = lax.broadcasted_iota(jnp.int32, (rows, LANES), 1)
    last = record_tiles - first

    def inside_record(j):
        value = magnitude[j * rows : (j + 1) * rows]
        if first + j == 0:
            return jnp.where(lane >= LANES - HALF_TAPS, value, 0.0)
        if j >= last:
            return jnp.where(lane < LANES - HALF_TAPS, value, 0.0) if j == last else jnp.zeros_like(value)
        return value

    magnitude = jnp.concatenate([inside_record(j) for j in range(blocks + 2)], axis=0)
    ones = jnp.where((offset >= 0) & (offset <= 2 * RADIUS), 1.0, 0.0).astype(jnp.bfloat16)
    high, low = split_bf16(magnitude)
    level = (dot_f32(windows(high), ones) + dot_f32(windows(low), ones)) * (1.0 / (2 * RADIUS + 1))
    filtered = both[: (blocks + 1) * rows, LANES:]
    whitened = filtered / (level + epsilon)

    shift = LANES - HALF_TAPS - RADIUS
    moved = pltpu.roll(whitened, LANES - shift, 1)
    lane = lax.broadcasted_iota(jnp.int32, (blocks * rows, LANES), 1)
    aligned = jnp.where(lane < LANES - shift, moved[: blocks * rows], moved[rows:])
    flat = jnp.concatenate([aligned[j * rows : (j + 1) * rows] for j in range(blocks)], axis=1)

    segments = flags_ref.shape[1]
    at = lax.broadcasted_iota(jnp.int32, (segments, blocks * LANES), 1) + first * LANES
    at -= SAMP * lax.broadcasted_iota(jnp.int32, (segments, blocks * LANES), 0)
    inside = jnp.where((at >= 0) & (at < SAMP), 1.0, 0.0).astype(jnp.bfloat16)
    kept = dot_f32(flags_ref[...].astype(jnp.float32).astype(jnp.bfloat16), inside)
    flat = (flat * kept).astype(jnp.bfloat16)

    source = lax.broadcasted_iota(jnp.int32, (2 * LANES, 2 * LANES), 0)
    target = lax.broadcasted_iota(jnp.int32, (2 * LANES, 2 * LANES), 1)
    wanted = jnp.where(target < LANES, 2 * target, 2 * target - 2 * LANES + 1)
    sort = jnp.where(source == wanted, 1.0, 0.0).astype(jnp.bfloat16)
    pairs = range(0, blocks * LANES, 2 * LANES)
    stacked = jnp.concatenate([flat[:, j : j + 2 * LANES] for j in pairs], axis=0)
    sorted_pairs = dot_f32(stacked, sort).astype(jnp.bfloat16)
    phases = [
        jnp.concatenate(
            [sorted_pairs[j * rows : (j + 1) * rows, at : at + LANES] for j in range(len(pairs))], axis=1
        )
        for at in (0, LANES)
    ]
    length = chunk_segs * SAMP // 2
    filling = jnp.zeros((rows, pl.cdiv(length, LANES) * LANES - length), jnp.bfloat16)
    for unit_starts, out_ref in zip(starts, out_refs):
        parts = []
        for start in unit_starts:
            at = (start - first * LANES) // 2
            for phase in phases:
                parts += [phase[:, at : at + length], filling]
        out_ref[...] = jnp.concatenate(parts, axis=1)


def whiten(traces, fir_taps, seg_flags, starts):
    rows, record_len = traces.shape
    vmem = pl.BlockSpec(memory_space=pltpu.VMEM)
    length = chunk_segs * SAMP
    window = 2 * pl.cdiv(length // 2, LANES) * LANES
    first = min(min(s) for s in starts) // LANES
    blocks = pl.cdiv(max(max(s) for s in starts) + length - first * LANES, 2 * LANES) * 2
    reach = min((first + blocks + 2) * LANES, record_len)
    return pl.pallas_call(
        functools.partial(whiten_kernel, record_len // LANES, first, blocks, starts),
        grid=(1,),
        in_specs=[
            pl.BlockSpec(memory_space=pltpu.SMEM),
            pl.BlockSpec((rows, reach), lambda step: (0, 0)),
            vmem,
        ],
        out_specs=[vmem] * len(starts),
        out_shape=[jax.ShapeDtypeStruct((rows, window * len(s)), jnp.bfloat16) for s in starts],
        compiler_params=pltpu.CompilerParams(vmem_limit_bytes=vmem_bytes),
        name="whiten",
    )(fir_taps, traces, seg_flags)


def route_kernel(count, place_ref, *refs):
    rows = refs[0].shape[0]
    outs = refs[-count:]
    for index, out_ref in enumerate(outs):
        for source_index, source in enumerate(refs[:count]):

            @pl.when(place_ref[index] == source_index)
            def _(source=source, out_ref=out_ref):
                out_ref[:rows, :] = source[...]

        if out_ref.shape[0] > rows:
            out_ref[rows:, :] = refs[count][...]


def route(place, parts, rows, extra):
    length = parts[0][0].shape[1]
    kind = parts[0][0].dtype

    def spec(count, at=0):
        return pl.BlockSpec((count, length), lambda step: (at, 0))

    counts = [rows] + [rows if extra is None else 2 * rows] * (len(parts) - 1)
    more = [] if extra is None else [extra]
    return pl.pallas_call(
        functools.partial(route_kernel, len(parts)),
        grid=(1,),
        in_specs=[pl.BlockSpec(memory_space=pltpu.SMEM)]
        + [spec(rows, at) for _, at in parts]
        + [spec(rows) for _ in more],
        out_specs=[spec(count) for count in counts],
        out_shape=[jax.ShapeDtypeStruct((count, length), kind) for count in counts],
        compiler_params=pltpu.CompilerParams(vmem_limit_bytes=24 << 20),
        name="route",
    )(place, *[array for array, _ in parts], *more)


def correlate_kernel(begins, left_rows, piece_rows, has_total, last, scale, place_ref, *refs):
    lefts, refs = refs[: len(begins)], list(refs[len(begins) :])
    staged = refs.pop() if piece_rows % 16 else None
    *refs, out_ref, even, odd, columns, both, shifted, edge, sems = refs
    mask_ref = refs.pop() if last else None
    total_ref = refs.pop() if has_total else None
    row_count, width = even.shape
    step = pl.program_id(0)
    lowest = SHIFTS // 2 + 1 - shift_group * (step + 1)

    @pl.when(step == 0)
    def _():
        copies = []

        def copy(source, target):
            copies.append(pltpu.make_async_copy(source, target, sems.at[len(copies)]))
            copies[-1].start()

        for index, (left, (row, begin)) in enumerate(zip(lefts, begins)):
            at, rows = pl.ds(index * left_rows, left_rows), pl.ds(row, left_rows)
            copy(left.at[rows, pl.ds(begin, width)], even.at[at])
            copy(left.at[rows, pl.ds(begin + width, width)], odd.at[at])
        for index, piece in enumerate(refs):
            at = pl.ds(pl.multiple_of(place_ref[index] * piece_rows, piece_rows), piece_rows)
            if staged is None:
                copy(piece.at[pl.ds(0, piece_rows)], columns.at[at])
            else:
                staged[at, :] = piece[...].astype(staged.dtype)
        if staged is not None:
            columns[...] = staged[...].astype(columns.dtype)
        for started in copies:
            started.wait()
        both[...] = columns[:, :width] + columns[:, width:]
        start = (SHIFTS // 2 + 1 - shift_group) % width
        even[...] = pltpu.roll(even[...], start, 1)
        odd[...] = pltpu.roll(odd[...], start, 1)
        edge[...] = jnp.zeros_like(edge)

    half = SAMP // 2
    sample = lax.broadcasted_iota(jnp.int32, (16, width), 1)
    phase = sample
    for segment in range(1, chunk_segs):
        phase = jnp.where(sample >= segment * half, sample - segment * half, phase)
    phase = jnp.where(sample >= chunk_segs * half, -SAMP, phase)

    def shift(base, index):
        move = lowest + index
        rolled = pltpu.roll(base, index, 1) if index else base
        keep = jnp.where((phase >= move) & (phase < half + move), 1.0, 0.0).astype(jnp.bfloat16)
        return rolled * jnp.concatenate([keep] * (row_count // 16), axis=0)

    base_even, base_odd = even[...], odd[...]
    for index in range(shift_group):
        rows = slice(index * row_count, (index + 1) * row_count)
        now = shift(base_even, index)
        shifted[0, rows, :] = now
        shifted[1, rows, :] = shift(base_odd, index)
        shifted[2, rows, :] = now + shift(base_odd, index + 1)
    even[...] = pltpu.roll(base_even, width - shift_group, 1)
    odd[...] = pltpu.roll(base_odd, width - shift_group, 1)
    rights = columns.at[:, :width], columns.at[:, width:], both
    products = []
    for index, right in enumerate(rights):
        value = lax.dot_general(
            shifted[index], right[...], (((1,), (1,)), ((), ())), preferred_element_type=jnp.float32
        ).reshape(shift_group, row_count, columns.shape[0])
        products.append(value + total_ref[index].astype(jnp.float32) if has_total else value)
    if not last:
        for index, value in enumerate(products):
            out_ref[index] = value.astype(out_ref.dtype)
        return
    zero, one, mixed = products
    higher = [one[index] for index in range(1, shift_group)] + [edge[...]]
    for index in range(len(lefts)):
        rows = slice(index * left_rows, (index + 1) * left_rows)
        at = pl.ds(pl.multiple_of(place_ref[len(refs) + index] * left_rows, left_rows), left_rows)
        weight = mask_ref[at, :].astype(jnp.float32) * scale
        for m in range(shift_group):
            out_ref[2 * m, at, :] = (zero[m, rows] + one[m, rows]) * weight
            out_ref[2 * m + 1, at, :] = (mixed[m, rows] - zero[m, rows] - higher[m][rows]) * weight
    edge[...] = one[0]


def correlate(place, lefts, begins, right, total, mask, last, scale):
    rows, cols = mask.shape
    left_rows, piece_rows = rows // len(lefts), cols // len(right)
    window = right[0].shape[1]
    width = window // 2
    steps = SHIFTS // shift_group
    any_space = pl.BlockSpec(memory_space=pl.ANY)
    whole = pl.BlockSpec((piece_rows, window), lambda step: (0, 0)) if piece_rows % 16 else any_space
    block = pl.BlockSpec((3, shift_group, rows, cols), lambda step: (0, steps - 1 - step, 0, 0))
    operands = [place, *lefts, *right]
    specs = [pl.BlockSpec(memory_space=pltpu.SMEM)] + [any_space] * len(lefts)
    specs += [whole] * len(right)
    aliases = {}
    if total is not None:
        if not last:
            aliases = {len(operands): 0}
        operands.append(total)
        specs.append(block)
    if last:
        operands.append(mask)
        specs.append(pl.BlockSpec((rows, cols), lambda step: (0, 0)))
        block = pl.BlockSpec((2 * shift_group, rows, cols), lambda step: (steps - 1 - step, 0, 0))
    scratch = [
        pltpu.VMEM((rows, width), jnp.bfloat16),
        pltpu.VMEM((rows, width), jnp.bfloat16),
        pltpu.VMEM((cols, window), jnp.bfloat16),
        pltpu.VMEM((cols, width), jnp.bfloat16),
        pltpu.VMEM((3, shift_group * rows, width), jnp.bfloat16),
        pltpu.VMEM((rows, cols), jnp.float32),
        pltpu.SemaphoreType.DMA((2 * len(lefts) + len(right),)),
    ]
    if piece_rows % 16:
        scratch.append(pltpu.VMEM((cols, window), jnp.float32))
    out_shape = (LAGS, rows, cols) if last else (3, SHIFTS, rows, cols)
    return pl.pallas_call(
        functools.partial(
            correlate_kernel, begins, left_rows, piece_rows, total is not None, last, scale
        ),
        grid=(steps,),
        in_specs=specs,
        out_specs=block,
        out_shape=jax.ShapeDtypeStruct(out_shape, jnp.float32 if last else jnp.bfloat16),
        input_output_aliases=aliases,
        scratch_shapes=scratch,
        compiler_params=pltpu.CompilerParams(vmem_limit_bytes=vmem_bytes if total is None else 34 << 20),
        name="correlate",
    )(*operands)


def body(traces, fir_taps, seg_flags, pair_mask):
    stn_count, seg_count = lax.axis_size("stn"), lax.axis_size("seg")
    sides = stn_count // seg_count
    stn, seg = lax.axis_index("stn"), lax.axis_index("seg")
    plane, side = stn // sides, stn % sides
    segments = seg_flags.shape[1]
    count = segments // chunk_segs
    scale = 1.0 / math.sqrt(SAMP * segments)
    partner = jnp.stack([seg ^ k for k in range(seg_count)]).astype(jnp.int32)
    route_place = plane ^ partner
    rows = traces.shape[0]
    place = [(side ^ j) * seg_count + partner for j in range(sides)]

    def to_seg(value, k):
        return lax.ppermute(value, "seg", [(i, i ^ k) for i in range(seg_count)])

    def to_plane(value, k):
        return lax.ppermute(value, "stn", [(i, i ^ (k * sides)) for i in range(stn_count)])

    def to_side(value, j):
        return lax.ppermute(value, "stn", [(i, i ^ j) for i in range(stn_count)])

    length = chunk_segs * SAMP
    half = count // 2
    starts = [u * length for u in range(count)]
    units = list(whiten(traces, fir_taps, seg_flags, [[0]]))
    several = [starts[1 : half + 1], starts[half:]]
    *rest, middle, late = whiten(traces, fir_taps, seg_flags, [[start] for start in starts[1:]] + several)
    units += rest
    window = units[0].shape[1]

    direct = [k for k in range(1, seg_count) if k & (k - 1) == 0][::-1]
    passed = [k for k in range(1, seg_count) if k & (k - 1)]
    gathered = rows % 16 > 0
    place.append(jnp.zeros((1,), jnp.int32) if gathered else partner)
    place = jnp.concatenate(place).astype(jnp.int32)

    state = {("unit", u): unit for u, unit in enumerate(units)}
    state["middle"], state["late"] = middle, late
    lines = [{0: (("unit", u), 0)} for u in range(count)]

    def fence():
        names = list(state)
        state.update(zip(names, lax.optimization_barrier([state[n] for n in names])))

    def value(u, k):
        name, at = lines[u][k]
        return state[name][at * rows : (at + 1) * rows] if at else state[name][:rows]

    def hop(k, *moves):
        sent = [value(u, slot ^ k) for u, slot in moves]
        name = ("line", *moves)
        state[name] = to_plane(jnp.concatenate(sent, axis=0) if len(sent) > 1 else sent[0], k)
        for at, (u, slot) in enumerate(moves):
            lines[u][slot] = name, at

    def plane_hops(u):
        ahead = u + 1 < count
        if len(passed) == 1 and u >= 0:
            if ahead:
                hop(direct[0], (u + 1, direct[0]))
            if u < count:
                hop(direct[1], *([(u, passed[0])] + ([(u + 1, direct[1])] if ahead else [])))
            return
        for k in passed if 0 <= u < count else []:
            hop(k & (k - 1), (u, k))
        for k in direct if ahead else []:
            hop(k, (u + 1, k))

    def columns(u, extra=None):
        parts = [(state[lines[u][k][0]], lines[u][k][1]) for k in range(seg_count)]
        more = None if extra is None else state["unit", extra]
        for k, piece in enumerate(route(route_place, parts, rows, more)):
            state["own", u, k] = to_seg(piece, k) if k else piece
            if k and extra is not None:
                rows_of[extra][k] = ("own", u, k), (rows, 0)

    rows_of = [{0: (("unit", u), (0, 0))} for u in range(count)]

    def row_hop(k, source, covered):
        name = ("row", k, source)
        state[name] = to_seg(state[source], k)
        for u in covered:
            rows_of[u][k] = name, (0, (u - covered[0]) * window)

    def gather_rows(source, covered):
        name = ("rows", source)
        state[name] = lax.all_gather(state[source], "seg", axis=0, tiled=True)
        for u in covered:
            rows_of[u] = {0: (name, (0, (u - covered[0]) * window))}

    def products(u):
        parts = [rows_of[u][k] for k in sorted(rows_of[u])]
        own = [state["own", u, k] for k in range(seg_count)]
        right = own + [to_side(v, j) for j in range(1, sides) for v in own]
        state["total"] = correlate(
            place,
            [state[name] for name, _ in parts],
            [begin for _, begin in parts],
            right,
            state.pop("total", None),
            pair_mask,
            u == count - 1,
            scale,
        )

    hops = list(range(1, seg_count))
    row_plan = {
        -1: [(k, ("unit", 0), [0]) for k in hops],
        0: [(k, "middle", range(1, half + 1)) for k in hops[:-1]] + [(hops[-1], ("unit", 1), [1])],
        half + 1: [(hops[-1], ("unit", half), [half])],
    }
    plane_hops(-1)
    if gathered:
        for source, covered in ((("unit", 0), [0]), ("middle", range(1, half)), ("late", range(half, count))):
            gather_rows(source, list(covered))
        row_plan = {}
    for u in range(-1, count + 2):
        if u >= 0:
            fence()
            plane_hops(u)
        if 1 <= u <= count:
            carried = u + 1 if half <= u < count - 1 and not gathered else None
            columns(u - 1, carried)
        for k, source, covered in row_plan.get(u, []):
            row_hop(k, source, list(covered))
        if 2 <= u <= count:
            products(u - 2)
    products(count - 1)
    return state["total"]


def solution(mesh):
    return jax.shard_map(
        body,
        mesh=mesh,
        in_specs=(P(("stn", "seg"), None), P(), P(("stn", "seg"), None), P("stn", "seg")),
        out_specs=P(None, "stn", "seg"),
        check_vma=False,
    )
```

```python
import functools
import math

import jax
import jax.numpy as jnp
from jax import lax
from jax.experimental import pallas as pl
from jax.experimental.pallas import tpu as pltpu
from jax.sharding import PartitionSpec as P

SAMP = 600
LAGS = 41
TAPS = 31
RADIUS = 64
LANES = 128
HALF_LAG = (LAGS - 1) // 2
SHIFTS = HALF_LAG + 1
HALF_TAPS = (TAPS - 1) // 2

epsilon = 1e-06
chunk_segs = 8
shift_group = 7
vmem_bytes = 58 << 20


def split_bf16(value):
    high = value.astype(jnp.bfloat16)
    low = (value - high.astype(jnp.float32)).astype(jnp.bfloat16)
    return high, low


def dot_f32(left, right):
    return jnp.dot(left, right, preferred_element_type=jnp.float32)


def whiten_kernel(record_tiles, first, blocks, starts, taps_ref, traces_ref, flags_ref, *out_refs):
    rows = traces_ref.shape[0]

    def tile(j):
        if j < 0 or j >= record_tiles:
            return jnp.zeros((rows, LANES), jnp.float32)
        return traces_ref[:, j * LANES : (j + 1) * LANES]

    stacked = jnp.concatenate([tile(first + j - 1) for j in range(blocks + 3)], axis=0)

    def windows(value):
        return jnp.concatenate([value[:-rows], value[rows:]], axis=1)

    offset = lax.broadcasted_iota(jnp.int32, (2 * LANES, LANES), 0) - lax.broadcasted_iota(
        jnp.int32, (2 * LANES, LANES), 1
    )
    band = jnp.zeros((2 * LANES, LANES), jnp.float32)
    for tap_index in range(TAPS):
        band = jnp.where(offset == tap_index, taps_ref[tap_index], band)
    late_band = jnp.concatenate(
        [jnp.zeros((RADIUS, LANES), jnp.float32), band[: 2 * LANES - RADIUS]], axis=0
    )
    band_high, band_low = split_bf16(jnp.concatenate([band, late_band], axis=1))
    high, low = split_bf16(stacked)
    high, low = windows(high), windows(low)
    both = dot_f32(high, band_high) + dot_f32(low, band_high) + dot_f32(high, band_low)

    magnitude = jnp.abs(both[:, :LANES])
    lane = lax.broadcasted_iota(jnp.int32, (rows, LANES), 1)
    last = record_tiles - first

    def inside_record(j):
        value = magnitude[j * rows : (j + 1) * rows]
        if first + j == 0:
            return jnp.where(lane >= LANES - HALF_TAPS, value, 0.0)
        if j >= last:
            return jnp.where(lane < LANES - HALF_TAPS, value, 0.0) if j == last else jnp.zeros_like(value)
        return value

    magnitude = jnp.concatenate([inside_record(j) for j in range(blocks + 2)], axis=0)
    ones = jnp.where((offset >= 0) & (offset <= 2 * RADIUS), 1.0, 0.0).astype(jnp.bfloat16)
    high, low = split_bf16(magnitude)
    level = (dot_f32(windows(high), ones) + dot_f32(windows(low), ones)) * (1.0 / (2 * RADIUS + 1))
    filtered = both[: (blocks + 1) * rows, LANES:]
    whitened = filtered / (level + epsilon)

    shift = LANES - HALF_TAPS - RADIUS
    moved = pltpu.roll(whitened, LANES - shift, 1)
    lane = lax.broadcasted_iota(jnp.int32, (blocks * rows, LANES), 1)
    aligned = jnp.where(lane < LANES - shift, moved[: blocks * rows], moved[rows:])
    flat = jnp.concatenate([aligned[j * rows : (j + 1) * rows] for j in range(blocks)], axis=1)

    segments = flags_ref.shape[1]
    at = lax.broadcasted_iota(jnp.int32, (segments, blocks * LANES), 1) + first * LANES
    at -= SAMP * lax.broadcasted_iota(jnp.int32, (segments, blocks * LANES), 0)
    inside = jnp.where((at >= 0) & (at < SAMP), 1.0, 0.0).astype(jnp.bfloat16)
    kept = dot_f32(flags_ref[...].astype(jnp.float32).astype(jnp.bfloat16), inside)
    flat = (flat * kept).astype(jnp.bfloat16)

    source = lax.broadcasted_iota(jnp.int32, (2 * LANES, 2 * LANES), 0)
    target = lax.broadcasted_iota(jnp.int32, (2 * LANES, 2 * LANES), 1)
    wanted = jnp.where(target < LANES, 2 * target, 2 * target - 2 * LANES + 1)
    sort = jnp.where(source == wanted, 1.0, 0.0).astype(jnp.bfloat16)
    pairs = range(0, blocks * LANES, 2 * LANES)
    stacked = jnp.concatenate([flat[:, j : j + 2 * LANES] for j in pairs], axis=0)
    sorted_pairs = dot_f32(stacked, sort).astype(jnp.bfloat16)
    phases = [
        jnp.concatenate(
            [sorted_pairs[j * rows : (j + 1) * rows, at : at + LANES] for j in range(len(pairs))], axis=1
        )
        for at in (0, LANES)
    ]
    length = chunk_segs * SAMP // 2
    filling = jnp.zeros((rows, pl.cdiv(length, LANES) * LANES - length), jnp.bfloat16)
    for unit_starts, out_ref in zip(starts, out_refs):
        parts = []
        for start in unit_starts:
            at = (start - first * LANES) // 2
            for phase in phases:
                parts += [phase[:, at : at + length], filling]
        out_ref[...] = jnp.concatenate(parts, axis=1)


def whiten(traces, fir_taps, seg_flags, starts):
    rows, record_len = traces.shape
    vmem = pl.BlockSpec(memory_space=pltpu.VMEM)
    length = chunk_segs * SAMP
    window = 2 * pl.cdiv(length // 2, LANES) * LANES
    first = min(min(s) for s in starts) // LANES
    blocks = pl.cdiv(max(max(s) for s in starts) + length - first * LANES, 2 * LANES) * 2
    reach = min((first + blocks + 2) * LANES, record_len)
    return pl.pallas_call(
        functools.partial(whiten_kernel, record_len // LANES, first, blocks, starts),
        grid=(1,),
        in_specs=[
            pl.BlockSpec(memory_space=pltpu.SMEM),
            pl.BlockSpec((rows, reach), lambda step: (0, 0)),
            vmem,
        ],
        out_specs=[vmem] * len(starts),
        out_shape=[jax.ShapeDtypeStruct((rows, window * len(s)), jnp.bfloat16) for s in starts],
        compiler_params=pltpu.CompilerParams(vmem_limit_bytes=vmem_bytes),
        name="whiten",
    )(fir_taps, traces, seg_flags)


def route_kernel(count, place_ref, *refs):
    rows = refs[0].shape[0]
    outs = refs[-count:]
    for index, out_ref in enumerate(outs):
        for source_index, source in enumerate(refs[:count]):

            @pl.when(place_ref[index] == source_index)
            def _(source=source, out_ref=out_ref):
                out_ref[:rows, :] = source[...]

        if out_ref.shape[0] > rows:
            out_ref[rows:, :] = refs[count][...]


def route(place, parts, rows, extra, longer):
    length = parts[0][0].shape[1]
    kind = parts[0][0].dtype

    def spec(count, at=0):
        return pl.BlockSpec((count, length), lambda step: (at, 0))

    counts = [2 * rows if k in longer else rows for k in range(len(parts))]
    more = [extra] if longer else []
    return pl.pallas_call(
        functools.partial(route_kernel, len(parts)),
        grid=(1,),
        in_specs=[pl.BlockSpec(memory_space=pltpu.SMEM)]
        + [spec(rows, at) for _, at in parts]
        + [spec(rows) for _ in more],
        out_specs=[spec(count) for count in counts],
        out_shape=[jax.ShapeDtypeStruct((count, length), kind) for count in counts],
        compiler_params=pltpu.CompilerParams(vmem_limit_bytes=24 << 20),
        name="route",
    )(place, *[array for array, _ in parts], *more)


def correlate_kernel(begins, left_rows, piece_rows, has_total, last, scale, place_ref, *refs):
    lefts, refs = refs[: len(begins)], list(refs[len(begins) :])
    staged = refs.pop() if piece_rows % 16 else None
    *refs, out_ref, even, odd, columns, both, shifted, edge, sems = refs
    mask_ref = refs.pop() if last else None
    total_ref = refs.pop() if has_total else None
    row_count, width = even.shape
    step = pl.program_id(0)
    lowest = SHIFTS // 2 + 1 - shift_group * (step + 1)

    @pl.when(step == 0)
    def _():
        copies = []

        def copy(source, target):
            copies.append(pltpu.make_async_copy(source, target, sems.at[len(copies)]))
            copies[-1].start()

        for index, (left, (row, begin)) in enumerate(zip(lefts, begins)):
            at, rows = pl.ds(index * left_rows, left_rows), pl.ds(row, left_rows)
            copy(left.at[rows, pl.ds(begin, width)], even.at[at])
            copy(left.at[rows, pl.ds(begin + width, width)], odd.at[at])
        for index, piece in enumerate(refs):
            at = pl.ds(pl.multiple_of(place_ref[index] * piece_rows, piece_rows), piece_rows)
            if staged is None:
                copy(piece.at[pl.ds(0, piece_rows)], columns.at[at])
            else:
                staged[at, :] = piece[...].astype(staged.dtype)
        if staged is not None:
            columns[...] = staged[...].astype(columns.dtype)
        edge[...] = jnp.zeros_like(edge)
        start = (SHIFTS // 2 + 1 - shift_group) % width
        for started in copies[: 2 * len(lefts)]:
            started.wait()
        even[...] = pltpu.roll(even[...], start, 1)
        odd[...] = pltpu.roll(odd[...], start, 1)
        for started in copies[2 * len(lefts) :]:
            started.wait()
        both[...] = columns[:, :width] + columns[:, width:]

    half = SAMP // 2
    sample = lax.broadcasted_iota(jnp.int32, (16, width), 1)
    phase = sample
    for segment in range(1, chunk_segs):
        phase = jnp.where(sample >= segment * half, sample - segment * half, phase)
    phase = jnp.where(sample >= chunk_segs * half, -SAMP, phase)

    def shift(base, index):
        move = lowest + index
        rolled = pltpu.roll(base, index, 1) if index else base
        keep = jnp.where((phase >= move) & (phase < half + move), 1.0, 0.0).astype(jnp.bfloat16)
        return rolled * jnp.concatenate([keep] * (row_count // 16), axis=0)

    base_even, base_odd = even[...], odd[...]
    for index in range(shift_group):
        rows = slice(index * row_count, (index + 1) * row_count)
        now = shift(base_even, index)
        shifted[0, rows, :] = now
        shifted[1, rows, :] = shift(base_odd, index)
        shifted[2, rows, :] = now + shift(base_odd, index + 1)
    even[...] = pltpu.roll(base_even, width - shift_group, 1)
    odd[...] = pltpu.roll(base_odd, width - shift_group, 1)
    rights = columns.at[:, :width], columns.at[:, width:], both
    products = []
    for index, right in enumerate(rights):
        value = lax.dot_general(
            shifted[index], right[...], (((1,), (1,)), ((), ())), preferred_element_type=jnp.float32
        ).reshape(shift_group, row_count, columns.shape[0])
        products.append(value + total_ref[index].astype(jnp.float32) if has_total else value)
    if not last:
        for index, value in enumerate(products):
            out_ref[index] = value.astype(out_ref.dtype)
        return
    zero, one, mixed = products
    higher = [one[index] for index in range(1, shift_group)] + [edge[...]]
    for index in range(len(lefts)):
        rows = slice(index * left_rows, (index + 1) * left_rows)
        at = pl.ds(pl.multiple_of(place_ref[len(refs) + index] * left_rows, left_rows), left_rows)
        weight = mask_ref[at, :].astype(jnp.float32) * scale
        for m in range(shift_group):
            out_ref[2 * m, at, :] = (zero[m, rows] + one[m, rows]) * weight
            out_ref[2 * m + 1, at, :] = (mixed[m, rows] - zero[m, rows] - higher[m][rows]) * weight
    edge[...] = one[0]


def correlate(place, lefts, begins, right, total, mask, last, scale):
    rows, cols = mask.shape
    left_rows, piece_rows = rows // len(lefts), cols // len(right)
    window = right[0].shape[1]
    width = window // 2
    steps = SHIFTS // shift_group
    any_space = pl.BlockSpec(memory_space=pl.ANY)
    whole = pl.BlockSpec((piece_rows, window), lambda step: (0, 0)) if piece_rows % 16 else any_space
    block = pl.BlockSpec((3, shift_group, rows, cols), lambda step: (0, steps - 1 - step, 0, 0))
    operands = [place, *lefts, *right]
    specs = [pl.BlockSpec(memory_space=pltpu.SMEM)] + [any_space] * len(lefts)
    specs += [whole] * len(right)
    aliases = {}
    if total is not None:
        if not last:
            aliases = {len(operands): 0}
        operands.append(total)
        specs.append(block)
    if last:
        operands.append(mask)
        specs.append(pl.BlockSpec((rows, cols), lambda step: (0, 0)))
        block = pl.BlockSpec((2 * shift_group, rows, cols), lambda step: (steps - 1 - step, 0, 0))
    scratch = [
        pltpu.VMEM((rows, width), jnp.bfloat16),
        pltpu.VMEM((rows, width), jnp.bfloat16),
        pltpu.VMEM((cols, window), jnp.bfloat16),
        pltpu.VMEM((cols, width), jnp.bfloat16),
        pltpu.VMEM((3, shift_group * rows, width), jnp.bfloat16),
        pltpu.VMEM((rows, cols), jnp.float32),
        pltpu.SemaphoreType.DMA((2 * len(lefts) + len(right),)),
    ]
    if piece_rows % 16:
        scratch.append(pltpu.VMEM((cols, window), jnp.float32))
    out_shape = (LAGS, rows, cols) if last else (3, SHIFTS, rows, cols)
    return pl.pallas_call(
        functools.partial(
            correlate_kernel, begins, left_rows, piece_rows, total is not None, last, scale
        ),
        grid=(steps,),
        in_specs=specs,
        out_specs=block,
        out_shape=jax.ShapeDtypeStruct(out_shape, jnp.float32 if last else jnp.bfloat16),
        input_output_aliases=aliases,
        scratch_shapes=scratch,
        compiler_params=pltpu.CompilerParams(vmem_limit_bytes=(58 if total is None else 51) << 20),
        name="correlate",
    )(*operands)


def body(traces, fir_taps, seg_flags, pair_mask):
    stn_count, seg_count = lax.axis_size("stn"), lax.axis_size("seg")
    sides = stn_count // seg_count
    stn, seg = lax.axis_index("stn"), lax.axis_index("seg")
    plane, side = stn // sides, stn % sides
    segments = seg_flags.shape[1]
    count = segments // chunk_segs
    scale = 1.0 / math.sqrt(SAMP * segments)
    partner = jnp.stack([seg ^ k for k in range(seg_count)]).astype(jnp.int32)
    route_place = plane ^ partner
    rows = traces.shape[0]
    place = [(side ^ j) * seg_count + partner for j in range(sides)]

    def to_seg(value, k):
        return lax.ppermute(value, "seg", [(i, i ^ k) for i in range(seg_count)])

    def to_plane(value, k):
        return lax.ppermute(value, "stn", [(i, i ^ (k * sides)) for i in range(stn_count)])

    def to_side(value, j):
        return lax.ppermute(value, "stn", [(i, i ^ j) for i in range(stn_count)])

    length = chunk_segs * SAMP
    half = count // 2
    starts = [u * length for u in range(count)]
    units = list(whiten(traces, fir_taps, seg_flags, [[0]]))
    several = [starts[1 : half + 1], starts[half:]]
    *rest, middle, late = whiten(traces, fir_taps, seg_flags, [[start] for start in starts[1:]] + several)
    units += rest
    window = units[0].shape[1]

    direct = [k for k in range(1, seg_count) if k & (k - 1) == 0][::-1]
    passed = [k for k in range(1, seg_count) if k & (k - 1)]
    gathered = rows % 16 > 0
    place.append(jnp.zeros((1,), jnp.int32) if gathered else partner)
    place = jnp.concatenate(place).astype(jnp.int32)

    state = {("unit", u): unit for u, unit in enumerate(units)}
    state["middle"], state["late"] = middle, late
    lines = [{0: (("unit", u), 0)} for u in range(count)]

    def fence():
        names = list(state)
        state.update(zip(names, lax.optimization_barrier([state[n] for n in names])))

    def value(u, k):
        name, at = lines[u][k]
        return state[name][at * rows : (at + 1) * rows] if at else state[name][:rows]

    def hop(k, *moves):
        sent = [value(u, slot ^ k) for u, slot in moves]
        name = ("line", *moves)
        state[name] = to_plane(jnp.concatenate(sent, axis=0) if len(sent) > 1 else sent[0], k)
        for at, (u, slot) in enumerate(moves):
            lines[u][slot] = name, at

    def plane_hops(u):
        ahead = u + 1 < count
        if len(passed) == 1 and u >= 0:
            if ahead:
                hop(direct[0], (u + 1, direct[0]))
            if u < count:
                hop(direct[1], *([(u, passed[0])] + ([(u + 1, direct[1])] if ahead else [])))
            return
        for k in passed if 0 <= u < count else []:
            hop(k & (k - 1), (u, k))
        for k in direct if ahead else []:
            hop(k, (u + 1, k))

    def columns(u, extra, longer):
        parts = [(state[lines[u][k][0]], lines[u][k][1]) for k in range(seg_count)]
        more = state["unit", extra] if longer else None
        for k, piece in enumerate(route(route_place, parts, rows, more, longer)):
            state["own", u, k] = to_seg(piece, k) if k else piece
            if k in longer:
                rows_of[extra][k] = ("own", u, k), (rows, 0)

    rows_of = [{0: (("unit", u), (0, 0))} for u in range(count)]

    def row_hop(k, source, covered):
        name = ("row", k, source)
        state[name] = to_seg(state[source], k)
        for u in covered:
            rows_of[u][k] = name, (0, (u - covered[0]) * window)

    def gather_rows(source, covered):
        name = ("rows", source)
        state[name] = lax.all_gather(state[source], "seg", axis=0, tiled=True)
        for u in covered:
            rows_of[u] = {0: (name, (0, (u - covered[0]) * window))}

    def products(u):
        parts = [rows_of[u][k] for k in sorted(rows_of[u])]
        own = [state["own", u, k] for k in range(seg_count)]
        right = own + [to_side(v, j) for j in range(1, sides) for v in own]
        state["total"] = correlate(
            place,
            [state[name] for name, _ in parts],
            [begin for _, begin in parts],
            right,
            state.pop("total", None),
            pair_mask,
            u == count - 1,
            scale,
        )

    hops = list(range(1, seg_count))
    row_plan = {
        -1: [(k, ("unit", 0), [0]) for k in hops],
        0: [(k, "middle", range(1, half + 1)) for k in hops[:-1]] + [(hops[-1], ("unit", 1), [1])],
    }
    carried = {0: (half, hops[-1:])}
    for v in range(half + 1, count):
        carried[v - 2] = v, hops[:-1]
        carried[v - 1] = v, hops[-1:]
    plane_hops(-1)
    if gathered:
        for source, covered in ((("unit", 0), [0]), ("middle", range(1, half)), ("late", range(half, count))):
            gather_rows(source, list(covered))
        row_plan, carried = {}, {}
    for u in range(-1, count + 2):
        if u >= 0:
            fence()
            plane_hops(u)
        if 1 <= u <= count:
            columns(u - 1, *carried.get(u - 1, (None, [])))
        for k, source, covered in row_plan.get(u, []):
            row_hop(k, source, list(covered))
        if 2 <= u <= count:
            products(u - 2)
    products(count - 1)
    return state["total"]


def solution(mesh):
    return jax.shard_map(
        body,
        mesh=mesh,
        in_specs=(P(("stn", "seg"), None), P(), P(("stn", "seg"), None), P("stn", "seg")),
        out_specs=P(None, "stn", "seg"),
        check_vma=False,
    )
```

```python
import functools
import math

import jax
import jax.numpy as jnp
from jax import lax
from jax.experimental import pallas as pl
from jax.experimental.pallas import tpu as pltpu
from jax.sharding import PartitionSpec as P

SAMP = 600
LAGS = 41
TAPS = 31
RADIUS = 64
LANES = 128
HALF_LAG = (LAGS - 1) // 2
SHIFTS = HALF_LAG + 1
HALF_TAPS = (TAPS - 1) // 2

epsilon = 1e-06
chunk_segs = 8
shift_group = 7
vmem_bytes = 58 << 20


def split_bf16(value):
    high = value.astype(jnp.bfloat16)
    low = (value - high.astype(jnp.float32)).astype(jnp.bfloat16)
    return high, low


def dot_f32(left, right):
    return jnp.dot(left, right, preferred_element_type=jnp.float32)


def whiten_kernel(record_tiles, first, blocks, starts, taps_ref, traces_ref, flags_ref, *out_refs):
    rows = traces_ref.shape[0]

    def tile(j):
        if j < 0 or j >= record_tiles:
            return jnp.zeros((rows, LANES), jnp.float32)
        return traces_ref[:, j * LANES : (j + 1) * LANES]

    stacked = jnp.concatenate([tile(first + j - 1) for j in range(blocks + 3)], axis=0)

    def windows(value):
        return jnp.concatenate([value[:-rows], value[rows:]], axis=1)

    offset = lax.broadcasted_iota(jnp.int32, (2 * LANES, LANES), 0) - lax.broadcasted_iota(
        jnp.int32, (2 * LANES, LANES), 1
    )
    band = jnp.zeros((2 * LANES, LANES), jnp.float32)
    for tap_index in range(TAPS):
        band = jnp.where(offset == tap_index, taps_ref[tap_index], band)
    late_band = jnp.concatenate(
        [jnp.zeros((RADIUS, LANES), jnp.float32), band[: 2 * LANES - RADIUS]], axis=0
    )
    band_high, band_low = split_bf16(jnp.concatenate([band, late_band], axis=1))
    high, low = split_bf16(stacked)
    high, low = windows(high), windows(low)
    both = dot_f32(high, band_high) + dot_f32(low, band_high) + dot_f32(high, band_low)

    magnitude = jnp.abs(both[:, :LANES])
    lane = lax.broadcasted_iota(jnp.int32, (rows, LANES), 1)
    last = record_tiles - first

    def inside_record(j):
        value = magnitude[j * rows : (j + 1) * rows]
        if first + j == 0:
            return jnp.where(lane >= LANES - HALF_TAPS, value, 0.0)
        if j >= last:
            return jnp.where(lane < LANES - HALF_TAPS, value, 0.0) if j == last else jnp.zeros_like(value)
        return value

    magnitude = jnp.concatenate([inside_record(j) for j in range(blocks + 2)], axis=0)
    ones = jnp.where((offset >= 0) & (offset <= 2 * RADIUS), 1.0, 0.0).astype(jnp.bfloat16)
    high, low = split_bf16(magnitude)
    level = (dot_f32(windows(high), ones) + dot_f32(windows(low), ones)) * (1.0 / (2 * RADIUS + 1))
    filtered = both[: (blocks + 1) * rows, LANES:]
    whitened = filtered / (level + epsilon)

    shift = LANES - HALF_TAPS - RADIUS
    moved = pltpu.roll(whitened, LANES - shift, 1)
    lane = lax.broadcasted_iota(jnp.int32, (blocks * rows, LANES), 1)
    aligned = jnp.where(lane < LANES - shift, moved[: blocks * rows], moved[rows:])
    flat = jnp.concatenate([aligned[j * rows : (j + 1) * rows] for j in range(blocks)], axis=1)

    segments = flags_ref.shape[1]
    at = lax.broadcasted_iota(jnp.int32, (segments, blocks * LANES), 1) + first * LANES
    at -= SAMP * lax.broadcasted_iota(jnp.int32, (segments, blocks * LANES), 0)
    inside = jnp.where((at >= 0) & (at < SAMP), 1.0, 0.0).astype(jnp.bfloat16)
    kept = dot_f32(flags_ref[...].astype(jnp.float32).astype(jnp.bfloat16), inside)
    flat = (flat * kept).astype(jnp.bfloat16)

    source = lax.broadcasted_iota(jnp.int32, (2 * LANES, 2 * LANES), 0)
    target = lax.broadcasted_iota(jnp.int32, (2 * LANES, 2 * LANES), 1)
    wanted = jnp.where(target < LANES, 2 * target, 2 * target - 2 * LANES + 1)
    sort = jnp.where(source == wanted, 1.0, 0.0).astype(jnp.bfloat16)
    pairs = range(0, blocks * LANES, 2 * LANES)
    stacked = jnp.concatenate([flat[:, j : j + 2 * LANES] for j in pairs], axis=0)
    sorted_pairs = dot_f32(stacked, sort).astype(jnp.bfloat16)
    phases = [
        jnp.concatenate(
            [sorted_pairs[j * rows : (j + 1) * rows, at : at + LANES] for j in range(len(pairs))], axis=1
        )
        for at in (0, LANES)
    ]
    length = chunk_segs * SAMP // 2
    filling = jnp.zeros((rows, pl.cdiv(length, LANES) * LANES - length), jnp.bfloat16)
    for unit_starts, out_ref in zip(starts, out_refs):
        parts = []
        for start in unit_starts:
            at = (start - first * LANES) // 2
            for phase in phases:
                parts += [phase[:, at : at + length], filling]
        out_ref[...] = jnp.concatenate(parts, axis=1)


def whiten(traces, fir_taps, seg_flags, starts):
    rows, record_len = traces.shape
    vmem = pl.BlockSpec(memory_space=pltpu.VMEM)
    length = chunk_segs * SAMP
    window = 2 * pl.cdiv(length // 2, LANES) * LANES
    first = min(min(s) for s in starts) // LANES
    blocks = pl.cdiv(max(max(s) for s in starts) + length - first * LANES, 2 * LANES) * 2
    reach = min((first + blocks + 2) * LANES, record_len)
    return pl.pallas_call(
        functools.partial(whiten_kernel, record_len // LANES, first, blocks, starts),
        grid=(1,),
        in_specs=[
            pl.BlockSpec(memory_space=pltpu.SMEM),
            pl.BlockSpec((rows, reach), lambda step: (0, 0)),
            vmem,
        ],
        out_specs=[vmem] * len(starts),
        out_shape=[jax.ShapeDtypeStruct((rows, window * len(s)), jnp.bfloat16) for s in starts],
        compiler_params=pltpu.CompilerParams(vmem_limit_bytes=vmem_bytes),
        name="whiten",
    )(fir_taps, traces, seg_flags)


def route_kernel(count, place_ref, *refs):
    rows = refs[0].shape[0]
    outs = refs[-count:]
    for index, out_ref in enumerate(outs):
        for source_index, source in enumerate(refs[:count]):

            @pl.when(place_ref[index] == source_index)
            def _(source=source, out_ref=out_ref):
                out_ref[:rows, :] = source[...]

        if out_ref.shape[0] > rows:
            out_ref[rows:, :] = refs[count][...]


def route(place, parts, rows, extra, longer):
    length = parts[0][0].shape[1]
    kind = parts[0][0].dtype

    def spec(count, at=0):
        return pl.BlockSpec((count, length), lambda step: (at, 0))

    counts = [2 * rows if k in longer else rows for k in range(len(parts))]
    more = [extra] if longer else []
    return pl.pallas_call(
        functools.partial(route_kernel, len(parts)),
        grid=(1,),
        in_specs=[pl.BlockSpec(memory_space=pltpu.SMEM)]
        + [spec(rows, at) for _, at in parts]
        + [spec(rows) for _ in more],
        out_specs=[spec(count) for count in counts],
        out_shape=[jax.ShapeDtypeStruct((count, length), kind) for count in counts],
        compiler_params=pltpu.CompilerParams(vmem_limit_bytes=24 << 20),
        name="route",
    )(place, *[array for array, _ in parts], *more)


def correlate_kernel(begins, left_rows, piece_rows, has_total, last, scale, place_ref, *refs):
    lefts, refs = refs[: len(begins)], list(refs[len(begins) :])
    staged = refs.pop() if piece_rows % 16 else None
    *refs, out_ref, even, odd, columns, both, shifted, edge, sems = refs
    mask_ref = refs.pop() if last else None
    total_ref = refs.pop() if has_total else None
    row_count, width = even.shape
    step = pl.program_id(0)
    lowest = SHIFTS // 2 + 1 - shift_group * (step + 1)

    @pl.when(step == 0)
    def _():
        copies = []

        def copy(source, target):
            copies.append(pltpu.make_async_copy(source, target, sems.at[len(copies)]))
            copies[-1].start()

        for index, (left, (row, begin)) in enumerate(zip(lefts, begins)):
            at, rows = pl.ds(index * left_rows, left_rows), pl.ds(row, left_rows)
            copy(left.at[rows, pl.ds(begin, width)], even.at[at])
            copy(left.at[rows, pl.ds(begin + width, width)], odd.at[at])
        for index, piece in enumerate(refs):
            at = pl.ds(pl.multiple_of(place_ref[index] * piece_rows, piece_rows), piece_rows)
            if staged is None:
                copy(piece.at[pl.ds(0, piece_rows)], columns.at[at])
            else:
                staged[at, :] = piece[...].astype(staged.dtype)
        if staged is not None:
            columns[...] = staged[...].astype(columns.dtype)
        edge[...] = jnp.zeros_like(edge)
        start = (SHIFTS // 2 + 1 - shift_group) % width
        for started in copies[: 2 * len(lefts)]:
            started.wait()
        even[...] = pltpu.roll(even[...], start, 1)
        odd[...] = pltpu.roll(odd[...], start, 1)
        for started in copies[2 * len(lefts) :]:
            started.wait()
        both[...] = columns[:, :width] + columns[:, width:]

    half = SAMP // 2
    sample = lax.broadcasted_iota(jnp.int32, (16, width), 1)
    phase = sample
    for segment in range(1, chunk_segs):
        phase = jnp.where(sample >= segment * half, sample - segment * half, phase)
    phase = jnp.where(sample >= chunk_segs * half, -SAMP, phase)

    def shift(base, index):
        move = lowest + index
        rolled = pltpu.roll(base, index, 1) if index else base
        keep = jnp.where((phase >= move) & (phase < half + move), 1.0, 0.0).astype(jnp.bfloat16)
        return rolled * jnp.concatenate([keep] * (row_count // 16), axis=0)

    base_even, base_odd = even[...], odd[...]
    for index in range(shift_group):
        rows = slice(index * row_count, (index + 1) * row_count)
        now = shift(base_even, index)
        shifted[0, rows, :] = now
        shifted[1, rows, :] = shift(base_odd, index)
        shifted[2, rows, :] = now + shift(base_odd, index + 1)
    even[...] = pltpu.roll(base_even, width - shift_group, 1)
    odd[...] = pltpu.roll(base_odd, width - shift_group, 1)
    rights = columns.at[:, :width], columns.at[:, width:], both
    products = []
    for index, right in enumerate(rights):
        value = lax.dot_general(
            shifted[index], right[...], (((1,), (1,)), ((), ())), preferred_element_type=jnp.float32
        ).reshape(shift_group, row_count, columns.shape[0])
        products.append(value + total_ref[index].astype(jnp.float32) if has_total else value)
    if not last:
        for index, value in enumerate(products):
            out_ref[index] = value.astype(out_ref.dtype)
        return
    zero, one, mixed = products
    higher = [one[index] for index in range(1, shift_group)] + [edge[...]]
    for index in range(len(lefts)):
        rows = slice(index * left_rows, (index + 1) * left_rows)
        at = pl.ds(pl.multiple_of(place_ref[len(refs) + index] * left_rows, left_rows), left_rows)
        weight = mask_ref[at, :].astype(jnp.float32) * scale
        for m in range(shift_group):
            out_ref[2 * m, at, :] = (zero[m, rows] + one[m, rows]) * weight
            out_ref[2 * m + 1, at, :] = (mixed[m, rows] - zero[m, rows] - higher[m][rows]) * weight
    edge[...] = one[0]


def correlate(place, lefts, begins, right, total, mask, last, scale):
    rows, cols = mask.shape
    left_rows, piece_rows = rows // len(lefts), cols // len(right)
    window = right[0].shape[1]
    width = window // 2
    steps = SHIFTS // shift_group
    any_space = pl.BlockSpec(memory_space=pl.ANY)
    whole = pl.BlockSpec((piece_rows, window), lambda step: (0, 0)) if piece_rows % 16 else any_space
    block = pl.BlockSpec((3, shift_group, rows, cols), lambda step: (0, steps - 1 - step, 0, 0))
    operands = [place, *lefts, *right]
    specs = [pl.BlockSpec(memory_space=pltpu.SMEM)] + [any_space] * len(lefts)
    specs += [whole] * len(right)
    aliases = {}
    if total is not None:
        if not last:
            aliases = {len(operands): 0}
        operands.append(total)
        specs.append(block)
    if last:
        operands.append(mask)
        specs.append(pl.BlockSpec((rows, cols), lambda step: (0, 0)))
        block = pl.BlockSpec((2 * shift_group, rows, cols), lambda step: (steps - 1 - step, 0, 0))
    scratch = [
        pltpu.VMEM((rows, width), jnp.bfloat16),
        pltpu.VMEM((rows, width), jnp.bfloat16),
        pltpu.VMEM((cols, window), jnp.bfloat16),
        pltpu.VMEM((cols, width), jnp.bfloat16),
        pltpu.VMEM((3, shift_group * rows, width), jnp.bfloat16),
        pltpu.VMEM((rows, cols), jnp.float32),
        pltpu.SemaphoreType.DMA((2 * len(lefts) + len(right),)),
    ]
    if piece_rows % 16:
        scratch.append(pltpu.VMEM((cols, window), jnp.float32))
    out_shape = (LAGS, rows, cols) if last else (3, SHIFTS, rows, cols)
    return pl.pallas_call(
        functools.partial(
            correlate_kernel, begins, left_rows, piece_rows, total is not None, last, scale
        ),
        grid=(steps,),
        in_specs=specs,
        out_specs=block,
        out_shape=jax.ShapeDtypeStruct(out_shape, jnp.float32 if last else jnp.bfloat16),
        input_output_aliases=aliases,
        scratch_shapes=scratch,
        compiler_params=pltpu.CompilerParams(vmem_limit_bytes=(53 if total is None else 51) << 20),
        name="correlate",
    )(*operands)


def body(traces, fir_taps, seg_flags, pair_mask):
    stn_count, seg_count = lax.axis_size("stn"), lax.axis_size("seg")
    sides = stn_count // seg_count
    stn, seg = lax.axis_index("stn"), lax.axis_index("seg")
    plane, side = stn // sides, stn % sides
    segments = seg_flags.shape[1]
    count = segments // chunk_segs
    scale = 1.0 / math.sqrt(SAMP * segments)
    partner = jnp.stack([seg ^ k for k in range(seg_count)]).astype(jnp.int32)
    route_place = plane ^ partner
    rows = traces.shape[0]
    place = [(side ^ j) * seg_count + partner for j in range(sides)]

    def to_seg(value, k):
        return lax.ppermute(value, "seg", [(i, i ^ k) for i in range(seg_count)])

    def to_plane(value, k):
        return lax.ppermute(value, "stn", [(i, i ^ (k * sides)) for i in range(stn_count)])

    def to_side(value, j):
        return lax.ppermute(value, "stn", [(i, i ^ j) for i in range(stn_count)])

    length = chunk_segs * SAMP
    half = count // 2
    starts = [u * length for u in range(count)]
    units = list(whiten(traces, fir_taps, seg_flags, [[0]]))
    several = [starts[1 : half + 1], starts[half:]]
    *rest, middle, late = whiten(traces, fir_taps, seg_flags, [[start] for start in starts[1:]] + several)
    units += rest
    window = units[0].shape[1]

    direct = [k for k in range(1, seg_count) if k & (k - 1) == 0][::-1]
    passed = [k for k in range(1, seg_count) if k & (k - 1)]
    gathered = rows % 16 > 0
    place.append(jnp.zeros((1,), jnp.int32) if gathered else partner)
    place = jnp.concatenate(place).astype(jnp.int32)

    state = {("unit", u): unit for u, unit in enumerate(units)}
    state["middle"], state["late"] = middle, late
    state["place"], state["route_place"] = place, route_place
    lines = [{0: (("unit", u), 0)} for u in range(count)]

    def fence():
        names = list(state)
        state.update(zip(names, lax.optimization_barrier([state[n] for n in names])))

    def value(u, k):
        name, at = lines[u][k]
        return state[name][at * rows : (at + 1) * rows] if at else state[name][:rows]

    def hop(k, *moves):
        sent = [value(u, slot ^ k) for u, slot in moves]
        name = ("line", *moves)
        state[name] = to_plane(jnp.concatenate(sent, axis=0) if len(sent) > 1 else sent[0], k)
        for at, (u, slot) in enumerate(moves):
            lines[u][slot] = name, at

    def plane_hops(u):
        ahead = u + 1 < count
        if len(passed) == 1 and u >= 0:
            if ahead:
                hop(direct[0], (u + 1, direct[0]))
            if u < count:
                hop(direct[1], *([(u, passed[0])] + ([(u + 1, direct[1])] if ahead else [])))
            return
        for k in passed if 0 <= u < count else []:
            hop(k & (k - 1), (u, k))
        for k in direct if ahead else []:
            hop(k, (u + 1, k))

    def columns(u, extra, longer):
        parts = [(state[lines[u][k][0]], lines[u][k][1]) for k in range(seg_count)]
        more = state["unit", extra] if longer else None
        for k, piece in enumerate(route(state["route_place"], parts, rows, more, longer)):
            state["own", u, k] = to_seg(piece, k) if k else piece
            if k in longer:
                rows_of[extra][k] = ("own", u, k), (rows, 0)

    rows_of = [{0: (("unit", u), (0, 0))} for u in range(count)]

    def row_hop(k, source, covered):
        name = ("row", k, source)
        state[name] = to_seg(state[source], k)
        for u in covered:
            rows_of[u][k] = name, (0, (u - covered[0]) * window)

    def gather_rows(source, covered):
        name = ("rows", source)
        state[name] = lax.all_gather(state[source], "seg", axis=0, tiled=True)
        for u in covered:
            rows_of[u] = {0: (name, (0, (u - covered[0]) * window))}

    def products(u):
        parts = [rows_of[u][k] for k in sorted(rows_of[u])]
        own = [state["own", u, k] for k in range(seg_count)]
        right = own + [to_side(v, j) for j in range(1, sides) for v in own]
        state["total"] = correlate(
            state["place"],
            [state[name] for name, _ in parts],
            [begin for _, begin in parts],
            right,
            state.pop("total", None),
            pair_mask,
            u == count - 1,
            scale,
        )

    hops = list(range(1, seg_count))
    row_plan = {
        -1: [(k, ("unit", 0), [0]) for k in hops],
        0: [(k, "middle", range(1, half + 1)) for k in hops[:-1]] + [(hops[-1], ("unit", 1), [1])],
    }
    carried = {0: (half, hops[-1:])}
    for v in range(half + 1, count):
        carried[v - 2] = v, hops[:-1]
        carried[v - 1] = v, hops[-1:]
    plane_hops(-1)
    if gathered:
        for source, covered in ((("unit", 0), [0]), ("middle", range(1, half)), ("late", range(half, count))):
            gather_rows(source, list(covered))
        row_plan, carried = {}, {}
    for u in range(-1, count + 2):
        if u >= 0:
            fence()
            plane_hops(u)
        if 1 <= u <= count:
            columns(u - 1, *carried.get(u - 1, (None, [])))
        for k, source, covered in row_plan.get(u, []):
            row_hop(k, source, list(covered))
        if 2 <= u <= count:
            products(u - 2)
    products(count - 1)
    return state["total"]


def solution(mesh):
    return jax.shard_map(
        body,
        mesh=mesh,
        in_specs=(P(("stn", "seg"), None), P(), P(("stn", "seg"), None), P("stn", "seg")),
        out_specs=P(None, "stn", "seg"),
        check_vma=False,
    )
```

```python
import functools
import math

import jax
import jax.numpy as jnp
from jax import lax
from jax.experimental import pallas as pl
from jax.experimental.pallas import tpu as pltpu
from jax.sharding import PartitionSpec as P

SAMP = 600
LAGS = 41
TAPS = 31
RADIUS = 64
LANES = 128
HALF_LAG = (LAGS - 1) // 2
SHIFTS = HALF_LAG + 1
HALF_TAPS = (TAPS - 1) // 2

epsilon = 1e-06
chunk_segs = 8
shift_group = 7
vmem_bytes = 58 << 20


def split_bf16(value):
    high = value.astype(jnp.bfloat16)
    low = (value - high.astype(jnp.float32)).astype(jnp.bfloat16)
    return high, low


def dot_f32(left, right):
    return jnp.dot(left, right, preferred_element_type=jnp.float32)


def whiten_kernel(record_tiles, first, blocks, starts, taps_ref, traces_ref, flags_ref, *out_refs):
    rows = traces_ref.shape[0]

    def tile(j):
        if j < 0 or j >= record_tiles:
            return jnp.zeros((rows, LANES), jnp.float32)
        return traces_ref[:, j * LANES : (j + 1) * LANES]

    stacked = jnp.concatenate([tile(first + j - 1) for j in range(blocks + 3)], axis=0)

    def windows(value):
        return jnp.concatenate([value[:-rows], value[rows:]], axis=1)

    offset = lax.broadcasted_iota(jnp.int32, (2 * LANES, LANES), 0) - lax.broadcasted_iota(
        jnp.int32, (2 * LANES, LANES), 1
    )
    band = jnp.zeros((2 * LANES, LANES), jnp.float32)
    for tap_index in range(TAPS):
        band = jnp.where(offset == tap_index, taps_ref[tap_index], band)
    late_band = jnp.concatenate(
        [jnp.zeros((RADIUS, LANES), jnp.float32), band[: 2 * LANES - RADIUS]], axis=0
    )
    band_high, band_low = split_bf16(jnp.concatenate([band, late_band], axis=1))
    high, low = split_bf16(stacked)
    high, low = windows(high), windows(low)
    both = dot_f32(high, band_high) + dot_f32(low, band_high) + dot_f32(high, band_low)

    magnitude = jnp.abs(both[:, :LANES])
    lane = lax.broadcasted_iota(jnp.int32, (rows, LANES), 1)
    last = record_tiles - first

    def inside_record(j):
        value = magnitude[j * rows : (j + 1) * rows]
        if first + j == 0:
            return jnp.where(lane >= LANES - HALF_TAPS, value, 0.0)
        if j >= last:
            return jnp.where(lane < LANES - HALF_TAPS, value, 0.0) if j == last else jnp.zeros_like(value)
        return value

    magnitude = jnp.concatenate([inside_record(j) for j in range(blocks + 2)], axis=0)
    ones = jnp.where((offset >= 0) & (offset <= 2 * RADIUS), 1.0, 0.0).astype(jnp.bfloat16)
    high, low = split_bf16(magnitude)
    level = (dot_f32(windows(high), ones) + dot_f32(windows(low), ones)) * (1.0 / (2 * RADIUS + 1))
    filtered = both[: (blocks + 1) * rows, LANES:]
    whitened = filtered / (level + epsilon)

    shift = LANES - HALF_TAPS - RADIUS
    moved = pltpu.roll(whitened, LANES - shift, 1)
    lane = lax.broadcasted_iota(jnp.int32, (blocks * rows, LANES), 1)
    aligned = jnp.where(lane < LANES - shift, moved[: blocks * rows], moved[rows:])
    flat = jnp.concatenate([aligned[j * rows : (j + 1) * rows] for j in range(blocks)], axis=1)

    segments = flags_ref.shape[1]
    at = lax.broadcasted_iota(jnp.int32, (segments, blocks * LANES), 1) + first * LANES
    at -= SAMP * lax.broadcasted_iota(jnp.int32, (segments, blocks * LANES), 0)
    inside = jnp.where((at >= 0) & (at < SAMP), 1.0, 0.0).astype(jnp.bfloat16)
    kept = dot_f32(flags_ref[...].astype(jnp.float32).astype(jnp.bfloat16), inside)
    flat = (flat * kept).astype(jnp.bfloat16)

    source = lax.broadcasted_iota(jnp.int32, (2 * LANES, 2 * LANES), 0)
    target = lax.broadcasted_iota(jnp.int32, (2 * LANES, 2 * LANES), 1)
    wanted = jnp.where(target < LANES, 2 * target, 2 * target - 2 * LANES + 1)
    sort = jnp.where(source == wanted, 1.0, 0.0).astype(jnp.bfloat16)
    pairs = range(0, blocks * LANES, 2 * LANES)
    stacked = jnp.concatenate([flat[:, j : j + 2 * LANES] for j in pairs], axis=0)
    sorted_pairs = dot_f32(stacked, sort).astype(jnp.bfloat16)
    phases = [
        jnp.concatenate(
            [sorted_pairs[j * rows : (j + 1) * rows, at : at + LANES] for j in range(len(pairs))], axis=1
        )
        for at in (0, LANES)
    ]
    length = chunk_segs * SAMP // 2
    filling = jnp.zeros((rows, pl.cdiv(length, LANES) * LANES - length), jnp.bfloat16)
    for unit_starts, out_ref in zip(starts, out_refs):
        parts = []
        for start in unit_starts:
            at = (start - first * LANES) // 2
            for phase in phases:
                parts += [phase[:, at : at + length], filling]
        out_ref[...] = jnp.concatenate(parts, axis=1)


def whiten(traces, fir_taps, seg_flags, starts):
    rows, record_len = traces.shape
    vmem = pl.BlockSpec(memory_space=pltpu.VMEM)
    length = chunk_segs * SAMP
    window = 2 * pl.cdiv(length // 2, LANES) * LANES
    first = min(min(s) for s in starts) // LANES
    blocks = pl.cdiv(max(max(s) for s in starts) + length - first * LANES, 2 * LANES) * 2
    reach = min((first + blocks + 2) * LANES, record_len)
    return pl.pallas_call(
        functools.partial(whiten_kernel, record_len // LANES, first, blocks, starts),
        grid=(1,),
        in_specs=[
            pl.BlockSpec(memory_space=pltpu.SMEM),
            pl.BlockSpec((rows, reach), lambda step: (0, 0)),
            vmem,
        ],
        out_specs=[vmem] * len(starts),
        out_shape=[jax.ShapeDtypeStruct((rows, window * len(s)), jnp.bfloat16) for s in starts],
        compiler_params=pltpu.CompilerParams(vmem_limit_bytes=vmem_bytes),
        name="whiten",
    )(fir_taps, traces, seg_flags)


def route_kernel(count, place_ref, *refs):
    rows = refs[0].shape[0]
    outs = refs[-count:]
    for index, out_ref in enumerate(outs):
        for source_index, source in enumerate(refs[:count]):

            @pl.when(place_ref[index] == source_index)
            def _(source=source, out_ref=out_ref):
                out_ref[:rows, :] = source[...]

        if out_ref.shape[0] > rows:
            out_ref[rows:, :] = refs[count][...]


def route(place, parts, rows, extra, longer):
    length = parts[0][0].shape[1]
    kind = parts[0][0].dtype

    def spec(count, at=0):
        return pl.BlockSpec((count, length), lambda step: (at, 0))

    counts = [2 * rows if k in longer else rows for k in range(len(parts))]
    more = [extra] if longer else []
    return pl.pallas_call(
        functools.partial(route_kernel, len(parts)),
        grid=(1,),
        in_specs=[pl.BlockSpec(memory_space=pltpu.SMEM)]
        + [spec(rows, at) for _, at in parts]
        + [spec(rows) for _ in more],
        out_specs=[spec(count) for count in counts],
        out_shape=[jax.ShapeDtypeStruct((count, length), kind) for count in counts],
        compiler_params=pltpu.CompilerParams(vmem_limit_bytes=24 << 20),
        name="route",
    )(place, *[array for array, _ in parts], *more)


def correlate_kernel(begins, left_rows, piece_rows, has_total, last, scale, place_ref, *refs):
    lefts, refs = refs[: len(begins)], list(refs[len(begins) :])
    staged = refs.pop() if piece_rows % 16 else None
    *refs, out_ref, even, odd, columns, both, shifted, edge, sems = refs
    mask_ref = refs.pop() if last else None
    total_ref = refs.pop() if has_total else None
    row_count, width = even.shape
    step = pl.program_id(0)
    lowest = SHIFTS // 2 + 1 - shift_group * (step + 1)

    @pl.when(step == 0)
    def _():
        copies = []

        def copy(source, target):
            copies.append(pltpu.make_async_copy(source, target, sems.at[len(copies)]))
            copies[-1].start()

        for index, (left, (row, begin)) in enumerate(zip(lefts, begins)):
            at, rows = pl.ds(index * left_rows, left_rows), pl.ds(row, left_rows)
            copy(left.at[rows, pl.ds(begin, width)], even.at[at])
            copy(left.at[rows, pl.ds(begin + width, width)], odd.at[at])
        for index, piece in enumerate(refs):
            at = pl.ds(pl.multiple_of(place_ref[index] * piece_rows, piece_rows), piece_rows)
            if staged is None:
                copy(piece.at[pl.ds(0, piece_rows)], columns.at[at])
            else:
                staged[at, :] = piece[...].astype(staged.dtype)
        if staged is not None:
            columns[...] = staged[...].astype(columns.dtype)
        edge[...] = jnp.zeros_like(edge)
        start = (SHIFTS // 2 + 1 - shift_group) % width
        for started in copies[: 2 * len(lefts)]:
            started.wait()
        even[...] = pltpu.roll(even[...], start, 1)
        odd[...] = pltpu.roll(odd[...], start, 1)
        for started in copies[2 * len(lefts) :]:
            started.wait()
        both[...] = columns[:, :width] + columns[:, width:]

    half = SAMP // 2
    sample = lax.broadcasted_iota(jnp.int32, (16, width), 1)
    phase = sample
    for segment in range(1, chunk_segs):
        phase = jnp.where(sample >= segment * half, sample - segment * half, phase)
    phase = jnp.where(sample >= chunk_segs * half, -SAMP, phase)

    def shift(base, index):
        move = lowest + index
        rolled = pltpu.roll(base, index, 1) if index else base
        keep = jnp.where((phase >= move) & (phase < half + move), 1.0, 0.0).astype(jnp.bfloat16)
        return rolled * jnp.concatenate([keep] * (row_count // 16), axis=0)

    base_even, base_odd = even[...], odd[...]
    for index in range(shift_group):
        rows = slice(index * row_count, (index + 1) * row_count)
        now = shift(base_even, index)
        shifted[0, rows, :] = now
        shifted[1, rows, :] = shift(base_odd, index)
        shifted[2, rows, :] = now + shift(base_odd, index + 1)
    even[...] = pltpu.roll(base_even, width - shift_group, 1)
    odd[...] = pltpu.roll(base_odd, width - shift_group, 1)
    rights = columns.at[:, :width], columns.at[:, width:], both
    products = []
    for index, right in enumerate(rights):
        value = lax.dot_general(
            shifted[index], right[...], (((1,), (1,)), ((), ())), preferred_element_type=jnp.float32
        ).reshape(shift_group, row_count, columns.shape[0])
        products.append(value + total_ref[index].astype(jnp.float32) if has_total else value)
    if not last:
        for index, value in enumerate(products):
            out_ref[index] = value.astype(out_ref.dtype)
        return
    zero, one, mixed = products
    higher = [one[index] for index in range(1, shift_group)] + [edge[...]]
    for index in range(len(lefts)):
        rows = slice(index * left_rows, (index + 1) * left_rows)
        at = pl.ds(pl.multiple_of(place_ref[len(refs) + index] * left_rows, left_rows), left_rows)
        weight = mask_ref[at, :].astype(jnp.float32) * scale
        for m in range(shift_group):
            out_ref[2 * m, at, :] = (zero[m, rows] + one[m, rows]) * weight
            out_ref[2 * m + 1, at, :] = (mixed[m, rows] - zero[m, rows] - higher[m][rows]) * weight
    edge[...] = one[0]


def correlate(place, lefts, begins, right, total, mask, last, scale):
    rows, cols = mask.shape
    left_rows, piece_rows = rows // len(lefts), cols // len(right)
    window = right[0].shape[1]
    width = window // 2
    steps = SHIFTS // shift_group
    any_space = pl.BlockSpec(memory_space=pl.ANY)
    whole = pl.BlockSpec((piece_rows, window), lambda step: (0, 0)) if piece_rows % 16 else any_space
    block = pl.BlockSpec((3, shift_group, rows, cols), lambda step: (0, steps - 1 - step, 0, 0))
    operands = [place, *lefts, *right]
    specs = [pl.BlockSpec(memory_space=pltpu.SMEM)] + [any_space] * len(lefts)
    specs += [whole] * len(right)
    aliases = {}
    if total is not None:
        if not last:
            aliases = {len(operands): 0}
        operands.append(total)
        specs.append(block)
    if last:
        operands.append(mask)
        specs.append(pl.BlockSpec((rows, cols), lambda step: (0, 0)))
        block = pl.BlockSpec((2 * shift_group, rows, cols), lambda step: (steps - 1 - step, 0, 0))
    scratch = [
        pltpu.VMEM((rows, width), jnp.bfloat16),
        pltpu.VMEM((rows, width), jnp.bfloat16),
        pltpu.VMEM((cols, window), jnp.bfloat16),
        pltpu.VMEM((cols, width), jnp.bfloat16),
        pltpu.VMEM((3, shift_group * rows, width), jnp.bfloat16),
        pltpu.VMEM((rows, cols), jnp.float32),
        pltpu.SemaphoreType.DMA((2 * len(lefts) + len(right),)),
    ]
    if piece_rows % 16:
        scratch.append(pltpu.VMEM((cols, window), jnp.float32))
    out_shape = (LAGS, rows, cols) if last else (3, SHIFTS, rows, cols)
    return pl.pallas_call(
        functools.partial(
            correlate_kernel, begins, left_rows, piece_rows, total is not None, last, scale
        ),
        grid=(steps,),
        in_specs=specs,
        out_specs=block,
        out_shape=jax.ShapeDtypeStruct(out_shape, jnp.float32 if last else jnp.bfloat16),
        input_output_aliases=aliases,
        scratch_shapes=scratch,
        compiler_params=pltpu.CompilerParams(vmem_limit_bytes=(53 if total is None else 51) << 20),
        name="correlate",
    )(*operands)


def body(traces, fir_taps, seg_flags, pair_mask):
    stn_count, seg_count = lax.axis_size("stn"), lax.axis_size("seg")
    sides = stn_count // seg_count
    stn, seg = lax.axis_index("stn"), lax.axis_index("seg")
    plane, side = stn // sides, stn % sides
    segments = seg_flags.shape[1]
    count = segments // chunk_segs
    scale = 1.0 / math.sqrt(SAMP * segments)
    partner = jnp.stack([seg ^ k for k in range(seg_count)]).astype(jnp.int32)
    route_place = plane ^ partner
    rows = traces.shape[0]
    place = [(side ^ j) * seg_count + partner for j in range(sides)]

    def to_seg(value, k):
        return lax.ppermute(value, "seg", [(i, i ^ k) for i in range(seg_count)])

    def to_plane(value, k):
        return lax.ppermute(value, "stn", [(i, i ^ (k * sides)) for i in range(stn_count)])

    def to_side(value, j):
        return lax.ppermute(value, "stn", [(i, i ^ j) for i in range(stn_count)])

    length = chunk_segs * SAMP
    half = count // 2
    starts = [u * length for u in range(count)]
    units = list(whiten(traces, fir_taps, seg_flags, [[0]]))
    gathered = rows % 16 > 0
    several = [starts[1 : half + 1]] + ([starts[half:]] if gathered else [])
    outs = whiten(traces, fir_taps, seg_flags, [[start] for start in starts[1:]] + several)
    units, several = units + list(outs[: count - 1]), outs[count - 1 :]
    window = units[0].shape[1]

    direct = [k for k in range(1, seg_count) if k & (k - 1) == 0][::-1]
    passed = [k for k in range(1, seg_count) if k & (k - 1)]
    place.append(jnp.zeros((1,), jnp.int32) if gathered else partner)
    place = jnp.concatenate(place).astype(jnp.int32)

    state = {("unit", u): unit for u, unit in enumerate(units)}
    state.update(zip(("middle", "late"), several))
    state["place"], state["route_place"] = place, route_place
    lines = [{0: (("unit", u), 0)} for u in range(count)]

    def fence():
        names = list(state)
        state.update(zip(names, lax.optimization_barrier([state[n] for n in names])))

    def value(u, k):
        name, at = lines[u][k]
        return state[name][at * rows : (at + 1) * rows] if at else state[name][:rows]

    def hop(k, *moves):
        sent = [value(u, slot ^ k) for u, slot in moves]
        name = ("line", *moves)
        state[name] = to_plane(jnp.concatenate(sent, axis=0) if len(sent) > 1 else sent[0], k)
        for at, (u, slot) in enumerate(moves):
            lines[u][slot] = name, at

    def plane_hops(u):
        ahead = u + 1 < count
        if len(passed) == 1 and u >= 0:
            if ahead:
                hop(direct[0], (u + 1, direct[0]))
            if u < count:
                hop(direct[1], *([(u, passed[0])] + ([(u + 1, direct[1])] if ahead else [])))
            return
        for k in passed if 0 <= u < count else []:
            hop(k & (k - 1), (u, k))
        for k in direct if ahead else []:
            hop(k, (u + 1, k))

    def columns(u, extra, longer):
        parts = [(state[lines[u][k][0]], lines[u][k][1]) for k in range(seg_count)]
        more = state["unit", extra] if longer else None
        for k, piece in enumerate(route(state["route_place"], parts, rows, more, longer)):
            state["own", u, k] = to_seg(piece, k) if k else piece
            if k in longer:
                rows_of[extra][k] = ("own", u, k), (rows, 0)

    rows_of = [{0: (("unit", u), (0, 0))} for u in range(count)]

    def row_hop(k, source, covered):
        name = ("row", k, source)
        state[name] = to_seg(state[source], k)
        for u in covered:
            rows_of[u][k] = name, (0, (u - covered[0]) * window)

    def gather_rows(source, covered):
        name = ("rows", source)
        state[name] = lax.all_gather(state[source], "seg", axis=0, tiled=True)
        for u in covered:
            rows_of[u] = {0: (name, (0, (u - covered[0]) * window))}

    def products(u):
        parts = [rows_of[u][k] for k in sorted(rows_of[u])]
        own = [state["own", u, k] for k in range(seg_count)]
        right = own + [to_side(v, j) for j in range(1, sides) for v in own]
        state["total"] = correlate(
            state["place"],
            [state[name] for name, _ in parts],
            [begin for _, begin in parts],
            right,
            state.pop("total", None),
            pair_mask,
            u == count - 1,
            scale,
        )

    hops = list(range(1, seg_count))
    row_plan = {
        -1: [(k, ("unit", 0), [0]) for k in hops],
        0: [(k, "middle", range(1, half + 1)) for k in hops[:-1]] + [(hops[-1], ("unit", 1), [1])],
    }
    carried = {0: (half, hops[-1:])}
    for v in range(half + 1, count):
        carried[v - 2] = v, hops[:-1]
        carried[v - 1] = v, hops[-1:]
    plane_hops(-1)
    if gathered:
        for source, covered in ((("unit", 0), [0]), ("middle", range(1, half)), ("late", range(half, count))):
            gather_rows(source, list(covered))
        row_plan, carried = {}, {}
    for u in range(-1, count + 2):
        if u >= 0:
            fence()
            plane_hops(u)
        if 1 <= u <= count:
            columns(u - 1, *carried.get(u - 1, (None, [])))
        for k, source, covered in row_plan.get(u, []):
            row_hop(k, source, list(covered))
        if 2 <= u <= count:
            products(u - 2)
    products(count - 1)
    return state["total"]


def solution(mesh):
    return jax.shard_map(
        body,
        mesh=mesh,
        in_specs=(P(("stn", "seg"), None), P(), P(("stn", "seg"), None), P("stn", "seg")),
        out_specs=P(None, "stn", "seg"),
        check_vma=False,
    )
```
